32 devices in a mesh: wide: 16 (over z, y, x), narrow: 2 (over core).
Axes of the slice: x: 2, y: 2, z: 4, core: 2. Of those that a mesh axis runs over, the one named last changes fastest.
Arguments:
- point_owner: int32 [32768, 1], P(('wide', 'narrow')), may hold values from 0 to 15; in each aligned block of 1024 rows (0 to 1023, 1024 to 2047, ...) at most 128 rows name the same one
- point_cell: int32 [32768], P(('wide', 'narrow')), may hold values from 0 to 8191
- normals: float32 [3, 32768], P(None, ('wide', 'narrow')), may hold values from -6 to 6
- strip_count: int32 [32], P(('wide', 'narrow')), may hold values from 1 to 1024, 28672 in all
- neighbours: int32 [16, 2, 2, 27], P('wide', 'narrow'), may hold values from 0 to 18, as said below
Outputs:
- solution: float32 [16, 2, 2, 4096], P('wide', 'narrow')
- residual: float32 [16, 2, 2, 4096], P('wide', 'narrow')
The draws below stay inside these ranges and needn't reach their ends.
Inputs may be any that keep to these rules, and one draw needn't show every extreme that they name: `point_owner`: the points of one device name each wide index at most 128 times, and some wide index exactly 128 times. `strip_count`: some device has exactly 1024 live points. `neighbours`: entries follow the encoding of the steps; dw and dn are -1, 0 or 1; the relation is mutual (b sees c in a direction exactly when c sees b in the opposite one); entry 13 names the brick itself.
All inputs are finite; a program needn't handle non-finite values.
Results may differ from the reference program's by a relative error of at most 0.0003.
Values sent between devices are 32-bit elements; how exact they have to be, the bound alone decides.
A program may use at most 64 MiB of HBM per device.

```python
import math
import jax
import jax.numpy as jnp
import numpy as np
from jax import lax

P_DEV = 1024
BR_DEV = 2
ITERS = 3
CAP = 128
POINTS = 32768
N_WIDE = 16
N_NARROW = 2


def draw_neighbours(key, part):
    device_count = N_WIDE * N_NARROW
    device = jnp.arange(device_count, dtype=jnp.int32)
    places = jax.vmap(lambda d: jax.random.permutation(jax.random.fold_in(key, d), 8))(device)[:, :BR_DEV].astype(jnp.int32)
    wide_at = (device // N_NARROW)[:, None]
    narrow_at = (device % N_NARROW)[:, None]
    coord_x = 2 * wide_at + places // 4
    coord_y = places // 2 % 2
    coord_z = 2 * narrow_at + places % 2
    slots = jnp.broadcast_to(jnp.arange(BR_DEV, dtype=jnp.int32)[None, :], places.shape)
    occupancy = jnp.full((2 * N_WIDE, 2, 2 * N_NARROW), -1, jnp.int32).at[coord_x, coord_y, coord_z].set(slots)
    steps_table = np.array([[a, b, c] for a in (-1, 0, 1) for b in (-1, 0, 1) for c in (-1, 0, 1)], np.int32)
    near_x = coord_x[:, :, None] + jnp.asarray(steps_table[:, 0])
    near_y = coord_y[:, :, None] + jnp.asarray(steps_table[:, 1])
    near_z = coord_z[:, :, None] + jnp.asarray(steps_table[:, 2])
    inside = (near_x >= 0) & (near_x < 2 * N_WIDE) & (near_y >= 0) & (near_y < 2) & (near_z >= 0) & (near_z < 2 * N_NARROW)
    found = occupancy[jnp.clip(near_x, 0, 2 * N_WIDE - 1), jnp.clip(near_y, 0, 1), jnp.clip(near_z, 0, 2 * N_NARROW - 1)]
    shift_w = jnp.clip(near_x, 0, 2 * N_WIDE - 1) // 2 - wide_at[:, :, None]
    shift_n = jnp.clip(near_z, 0, 2 * N_NARROW - 1) // 2 - narrow_at[:, :, None]
    encoded = ((shift_w + 1) * 3 + shift_n + 1) * BR_DEV + found
    encoded = jnp.where(inside & (found >= 0), encoded, 9 * BR_DEV)
    return encoded.reshape(N_WIDE, N_NARROW, BR_DEV, 27).astype(jnp.int32)


def touch_ends(drawn, key, low, largest):
    shape = drawn.shape
    index_at = [jax.random.randint(jax.random.fold_in(key, axis), (), 0, shape[axis]) for axis in range(len(shape))]
    drawn = drawn.at[tuple(index_at)].set(low)
    longest = shape.index(max(shape))
    index_at[longest] = (index_at[longest] + 1) % shape[longest]
    return drawn.at[tuple(index_at)].set(largest)


def levels(own_key, extent, pieces, smallest, top_value):
    def one(dim, blocks):
        steps = jax.random.uniform(jax.random.fold_in(jax.random.fold_in(own_key, 6), dim), (blocks,), jnp.float32, smallest / len(pieces), top_value / len(pieces))
        return jnp.repeat(jnp.exp(steps), extent[dim] // blocks).reshape((-1,) + (1,) * (len(extent) - dim - 1))

    gain = one(*pieces[0])
    for cut in pieces[1:]:
        gain = gain * one(*cut)
    return gain


def profile(amount, total, limit, lean):
    portions = [(1 << 20) // math.isqrt(grade ** lean) + 1 for grade in range(2, amount + 1)]
    rest, given = total - limit - (amount - 1), [1] * (amount - 1)
    while rest > 0:
        movable = [i for i in range(amount - 1) if given[i] < limit]
        mass, remaining = sum([portions[i] for i in movable]), rest
        for i in movable:
            extra = min(limit - given[i], max(1, remaining * portions[i] // mass), rest)
            given[i] = given[i] + extra
            rest = rest - extra
    return np.array([limit] + given)


def uneven(rng, number_of, total, most, slope):
    if number_of == 2:
        one = jax.random.randint(rng, (), max(1, total - most), min(most, total - 1) + 1)
        return jnp.stack([one, total - one])
    sizes = jnp.asarray(profile(number_of, total, most, slope), jnp.int32)
    twos = (number_of - 1) // 2
    source_of, receiver = sizes[1:1 + 2 * twos:2], sizes[2:2 + 2 * twos:2]
    margin = jnp.minimum(source_of - 1, most - receiver)
    moved = jax.random.randint(jax.random.fold_in(rng, 1), (twos,), 0, 1 << 20) % (margin + 1)
    sizes = sizes.at[1:1 + 2 * twos:2].set(source_of - moved).at[2:2 + 2 * twos:2].set(receiver + moved)
    return sizes[jax.random.permutation(jax.random.fold_in(rng, 2), number_of)]


def routed_block(key, own, number, rows, amount, top, most, lean):
    order = jax.random.permutation(key, amount)
    crowded, common = load_shares(amount, rows * top, most, lean, True), load_shares(amount, rows * top, most, lean, False)
    places = jnp.arange(amount)

    def named(sizes, turn):
        used = int((sizes > 0).sum())
        fixed = max(1, used // 4)
        shifted = fixed + (places - fixed + turn * (used - fixed)) % max(1, amount - fixed)
        return jnp.zeros((amount,), jnp.int32).at[order[jnp.where(places < fixed, places, shifted)]].set(jnp.asarray(sizes, jnp.int32))

    sizes = jnp.where(number % 4 == 0, named(crowded, number // 4), named(common, number - number // 4 - 1))
    mixed = jax.random.permutation(jax.random.fold_in(own, 3), amount)
    donor, sink = mixed[0:amount // 2 * 2:2], mixed[1:amount // 2 * 2:2]
    room = jnp.minimum(sizes[donor] - 1, most - sizes[sink]) // 2
    room = jnp.where((donor == order[0]) | (sink == order[0]) | (sizes[sink] == 0), 0, jnp.maximum(room, 0))
    shifted = jax.random.randint(jax.random.fold_in(own, 4), (amount // 2,), 0, 1 << 20) % (room + 1)
    sizes = sizes.at[donor].add(-shifted).at[sink].add(shifted)
    members = jnp.searchsorted(jnp.cumsum(sizes), jnp.arange(rows * top), side="right").astype(jnp.int32)
    grid = members.reshape(top, rows).T
    grid = grid[jax.random.permutation(jax.random.fold_in(own, 1), rows)]
    turn = jax.random.randint(jax.random.fold_in(own, 2), (rows, 1), 0, top)
    return jnp.take_along_axis(grid, (jnp.arange(top)[None, :] + turn) % top, axis=1)


def load_shares(number_of, total, most, lean, full):
    portions = [(1 << 20) // math.isqrt(standing ** lean) + 1 for standing in range(1, number_of + 1)]
    largest = most if full else min(most, max(-(-total // number_of), total * portions[0] // sum(portions)))
    least = 1 if total - largest >= number_of - 1 else 0
    counts, surplus = [largest] + [least] * (number_of - 1), total - largest - least * (number_of - 1)
    while surplus > 0:
        movable = [i for i in range(1, number_of) if counts[i] < largest] or [i for i in range(1, number_of) if counts[i] < most]
        pool, budget = sum([portions[i] for i in movable]), surplus
        for i in movable:
            addition = min(most - counts[i], max(1, budget * portions[i] // pool), surplus)
            counts[i] = counts[i] + addition
            surplus = surplus - addition
    return np.array(counts)


def noise(own_key, extent, scale, bound, cuts=(), kind=jnp.bfloat16):
    result = jax.random.normal(own_key, extent, jnp.float32) * scale
    if len(cuts) > 0:
        result = levels(own_key, extent, cuts, -0.22, 0.18) * result
    return jnp.clip(result, min=-bound, max=bound).astype(kind)


def setup_inputs(seed: int = 0) -> dict:
    streams_of = jax.random.split(jax.random.key(seed), 6)
    point_owner_keys = jax.random.split(jax.random.fold_in(streams_of[0], 1), POINTS // P_DEV)
    point_owner_turns = jax.random.permutation(jax.random.fold_in(streams_of[0], 3), POINTS // P_DEV)
    point_owner = jax.vmap(lambda own, number: routed_block(jax.random.fold_in(streams_of[0], 2), own, number, P_DEV, N_WIDE, 1, CAP, 2))(point_owner_keys, point_owner_turns).reshape((POINTS, 1))
    point_cell = touch_ends(jax.random.randint(streams_of[1], (POINTS,), 0, BR_DEV * 4096), jax.random.fold_in(streams_of[1], 1), 0, (BR_DEV * 4096) - 1).astype(jnp.int32)
    normals = noise(streams_of[2], (3, POINTS), 1.0, 6.0, ((1, 32),), jnp.float32)
    strip_count = uneven(streams_of[3], N_WIDE * N_NARROW, N_WIDE * N_NARROW * P_DEV * 7 // 8, P_DEV, 2).astype(jnp.int32)
    neighbours = draw_neighbours(jax.random.fold_in(streams_of[5], 71), 0)
    return {"point_owner": point_owner, "point_cell": point_cell, "normals": normals, "strip_count": strip_count, "neighbours": neighbours}


WEIGHTS = (0.0, 1.0, 0.5, 0.25)
DIRECTIONS = tuple((a, b, c) for a in (-1, 0, 1) for b in (-1, 0, 1) for c in (-1, 0, 1))


def cell_span(shift_by):
    if shift_by == -1:
        return 15, 16
    if shift_by == 1:
        return 0, 1
    return 0, 16


def fetch_piece(source, brick_table, step_x, step_y, step_z):
    column = (step_x + 1) * 9 + (step_y + 1) * 3 + (step_z + 1)
    low_x, high_x = cell_span(step_x)
    low_y, high_y = cell_span(step_y)
    low_z, high_z = cell_span(step_z)
    piece = source[:, low_x:high_x, low_y:high_y, low_z:high_z]
    return jnp.take(piece, brick_table[:, column], axis=0)


def make_source(rim_data):
    flat_rows = rim_data.reshape(-1, 4096)
    flat_rows = jnp.concatenate([flat_rows, jnp.zeros((1, 4096), flat_rows.dtype)], 0)
    return flat_rows.reshape(-1, 16, 16, 16)


def stencil(source, brick_table, values, diagonal):
    brick_count = values.shape[0]
    own_cube = values.reshape(brick_count, 16, 16, 16)
    planes = []
    for step_x in (-1, 0, 1):
        row_parts = []
        for step_y in (-1, 0, 1):
            col_parts = []
            for step_z in (-1, 0, 1):
                if step_x == 0 and step_y == 0 and step_z == 0:
                    col_parts.append(own_cube)
                else:
                    col_parts.append(fetch_piece(source, brick_table, step_x, step_y, step_z))
            row_parts.append(jnp.concatenate(col_parts, 3))
        planes.append(jnp.concatenate(row_parts, 2))
    padded = jnp.concatenate(planes, 1)
    summed = jnp.zeros_like(own_cube)
    for step_x, step_y, step_z in DIRECTIONS:
        reach = abs(step_x) + abs(step_y) + abs(step_z)
        if reach > 0:
            summed = summed + WEIGHTS[reach] * padded[:, 1 + step_x:17 + step_x, 1 + step_y:17 + step_y, 1 + step_z:17 + step_z]
    return diagonal * values - summed.reshape(brick_count, 4096)


def divergence(sources, brick_table, vector_field):
    brick_count = vector_field.shape[1]
    summed = jnp.zeros((brick_count, 16, 16, 16), vector_field.dtype)
    for direction in range(3):
        upper_step = [0, 0, 0]
        upper_step[direction] = 1
        lower_step = [0, 0, 0]
        lower_step[direction] = -1
        lower_piece = fetch_piece(sources[direction], brick_table, *lower_step)
        upper_piece = fetch_piece(sources[direction], brick_table, *upper_step)
        own_cube = vector_field[direction].reshape(brick_count, 16, 16, 16)
        extended = jnp.concatenate([lower_piece, own_cube, upper_piece], direction + 1)
        change = lax.slice_in_dim(extended, 2, 18, axis=direction + 1) - lax.slice_in_dim(extended, 0, 16, axis=direction + 1)
        summed = summed + change
    return -4.0 * summed.reshape(brick_count, 4096)


def reference(point_owner, point_cell, normals, strip_count, neighbours):
    device_count = N_WIDE * N_NARROW
    brick_cells = BR_DEV * 4096
    point_index = jnp.arange(POINTS, dtype=jnp.int32)
    device_of = point_index // P_DEV
    is_live = (point_index % P_DEV) < jnp.take(strip_count, device_of)
    owner_device = point_owner[:, 0] * N_NARROW + device_of % N_NARROW
    flat_cell = owner_device * brick_cells + point_cell
    weight_live = is_live.astype(jnp.float32)
    segments = device_count * brick_cells
    vector_field = jnp.stack([jax.ops.segment_sum(normals[c] * weight_live, flat_cell, num_segments=segments) for c in range(3)])
    vector_field = vector_field.reshape(3, N_WIDE, N_NARROW, BR_DEV, 4096)
    density = jax.ops.segment_sum(weight_live, flat_cell, num_segments=segments).reshape(N_WIDE, N_NARROW, BR_DEV, 4096)
    diagonal = 14.5 + 2.0 * density
    devices = jnp.arange(device_count, dtype=jnp.int32)

    padded_vectors = jnp.pad(vector_field, ((0, 0), (1, 1), (1, 1), (0, 0), (0, 0)))

    def source_at(device):
        wide_at = (device // N_NARROW).astype(jnp.int32)
        narrow_at = (device % N_NARROW).astype(jnp.int32)
        zero = jnp.zeros((), jnp.int32)
        sources = [make_source(lax.dynamic_slice(padded_vectors[c], (wide_at, narrow_at, zero, zero), (3, 3, BR_DEV, 4096))) for c in range(3)]
        return divergence(sources, neighbours[wide_at, narrow_at], vector_field[:, wide_at, narrow_at])

    right_side = lax.map(source_at, devices).reshape(N_WIDE, N_NARROW, BR_DEV, 4096)

    def apply_operator(values):
        padded = jnp.pad(values, ((1, 1), (1, 1), (0, 0), (0, 0)))

        def apply_at(device):
            wide_at = (device // N_NARROW).astype(jnp.int32)
            narrow_at = (device % N_NARROW).astype(jnp.int32)
            zero = jnp.zeros((), jnp.int32)
            source = make_source(lax.dynamic_slice(padded, (wide_at, narrow_at, zero, zero), (3, 3, BR_DEV, 4096)))
            return stencil(source, neighbours[wide_at, narrow_at], values[wide_at, narrow_at], diagonal[wide_at, narrow_at])

        return lax.map(apply_at, devices).reshape(N_WIDE, N_NARROW, BR_DEV, 4096)

    solution = jnp.zeros_like(right_side)
    residual = right_side
    direction = right_side
    norm_now = jnp.sum(residual * residual)
    for iteration in range(ITERS):
        image_field = apply_operator(direction)
        step_size = norm_now / jnp.sum(direction * image_field)
        solution = solution + step_size * direction
        residual = residual - step_size * image_field
        norm_next = jnp.sum(residual * residual)
        direction = residual + (norm_next / norm_now) * direction
        norm_now = norm_next
    return solution, residual
```

```python
import functools

import jax
import jax.numpy as jnp
from jax import lax
from jax.experimental import pallas as pl
from jax.experimental.pallas import tpu as pltpu
from jax.sharding import PartitionSpec as P

MESH = pl.DeviceIdType.MESH
NT = (((1,), (1,)), ((), ()))
F32 = jnp.float32
BF16 = jnp.bfloat16


def split3(values):
    high = values.astype(BF16).astype(F32)
    rest = values - high
    middle = rest.astype(BF16).astype(F32)
    return high, middle, rest - middle


def lanes(rows):
    lane = lax.broadcasted_iota(jnp.int32, (rows, 256), 1)
    return lane // 16, lane % 16


def kernel(
    wides, narrows, owner_ref, cell_ref, normal_ref, count_ref, near_ref, solution_ref, residual_ref,
    point_rows, point_out, point_in, vector_src, field_0, field_1, field_2, part_out, part_in,
    point_send, point_recv, halo_send, halo_recv, part_send, part_recv,
):
    field_src = (field_0, field_1, field_2)
    devices = wides * narrows
    wide = lax.axis_index("wide")
    narrow = lax.axis_index("narrow")
    me = wide * narrows + narrow
    points = cell_ref.shape[1]
    slots = point_out.shape[2]
    barrier = pltpu.get_barrier_semaphore()

    @pl.loop(1, devices)
    def _(k):
        other = lax.rem(me + k, devices)
        pl.semaphore_signal(
            barrier, inc=1, device_id=(other // narrows, lax.rem(other, narrows)), device_id_type=MESH
        )

    offsets = [(a, b) for a in (-1, 0, 1) for b in (-1, 0, 1) if (a, b) != (0, 0)]

    def inside(a, b):
        return (wide + a >= 0) & (wide + a < wides) & (narrow + b >= 0) & (narrow + b < narrows)

    vector_src[18] = jnp.zeros((3, 16, 256), F32)
    for turn in range(3):
        field_src[turn][18] = jnp.zeros((16, 256), F32)
    for a, b in offsets:
        place = (a + 1) * 3 + b + 1

        @pl.when(jnp.logical_not(inside(a, b)))
        def _(place=place):
            vector_src[2 * place : 2 * place + 2] = jnp.zeros((2, 3, 16, 256), F32)
            for turn in range(3):
                field_src[turn][2 * place : 2 * place + 2] = jnp.zeros((2, 16, 256), F32)

    owner = owner_ref[...]
    live = lax.broadcasted_iota(jnp.int32, (1, points), 1) < count_ref[0]
    owner_hot = jnp.where(
        lax.broadcasted_iota(jnp.int32, (wides, points), 0) == owner, 1.0, 0.0
    )
    blocks = points // 128
    stacked = jnp.concatenate([owner_hot[:, k * 128 : (k + 1) * 128] for k in range(blocks)], 0)
    earlier = jnp.where(
        lax.broadcasted_iota(jnp.int32, (128, 256), 0) < lax.broadcasted_iota(jnp.int32, (128, 256), 1),
        1.0,
        0.0,
    )
    counted = jnp.dot(stacked.astype(BF16), earlier.astype(BF16), preferred_element_type=F32)
    ranks = []
    before = jnp.zeros((wides, 128), F32)
    for k in range(blocks):
        rows = slice(k * wides, (k + 1) * wides)
        ranks.append(
            jnp.sum(stacked[rows] * (counted[rows, :128] + before), axis=0, keepdims=True)
        )
        before = before + counted[rows, 128:]
    slot = jnp.concatenate(ranks, 1).astype(jnp.int32) + owner * slots

    point_rows[0:3] = normal_ref[...]
    point_rows[3:4] = jnp.where(live, cell_ref[...] + 1, 0).astype(F32)
    point_rows[4:8] = jnp.zeros((4, points), F32)
    split_rows = jnp.concatenate(
        split3(point_rows[...]) + (jnp.zeros((8, points), F32),), 0
    ).astype(BF16)
    joined = 2 if slots % 128 == 0 and wides % 2 == 0 else 1
    slot_row = lax.broadcasted_iota(jnp.int32, (joined * slots, points), 0)
    for k in range(0, wides, joined):
        hot = jnp.where(slot_row == slot - k * slots, 1.0, 0.0).astype(BF16)
        moved = lax.dot_general(split_rows, hot, NT, preferred_element_type=F32)
        moved = moved[0:8] + moved[8:16] + moved[16:24]
        for j in range(joined):
            point_out[k + j] = moved[:, j * slots : (j + 1) * slots]

    pl.semaphore_wait(barrier, devices - 1)

    @pl.loop(1, wides)
    def _(k):
        other = lax.rem(wide + k, wides)
        pltpu.make_async_remote_copy(
            src_ref=point_out.at[other],
            dst_ref=point_in.at[wide],
            send_sem=point_send.at[0],
            recv_sem=point_recv.at[0],
            device_id=(other, narrow),
            device_id_type=MESH,
        ).start()

    point_in[pl.ds(wide, 1)] = point_out[pl.ds(wide, 1)]
    arrived = point_in.at[pl.ds(0, wides - 1)]
    pltpu.make_async_copy(arrived, arrived, point_recv.at[0]).wait()

    group = 8 if slots % 128 == 0 and wides % 8 == 0 else 1
    splatted = jnp.zeros((320, 256), F32)
    for k in range(0, wides, group):
        got = jnp.concatenate([point_in[k + j] for j in range(group)], 1)
        width = group * slots
        cell = got[3:4].astype(jnp.int32) - 1
        row_hot = lax.broadcasted_iota(jnp.int32, (32, width), 0) == lax.shift_right_arithmetic(cell, 8)
        lane_hot = lax.broadcasted_iota(jnp.int32, (256, width), 0) == (cell & 255)
        weights = []
        for c in range(3):
            weights.extend(split3(got[c : c + 1]))
        weights.append(jnp.ones((1, width), F32))
        weighted = jnp.concatenate([jnp.where(row_hot, w, 0.0) for w in weights], 0).astype(BF16)
        splatted = splatted + lax.dot_general(
            weighted, jnp.where(lane_hot, 1.0, 0.0).astype(BF16), NT, preferred_element_type=F32
        )
    vectors = [
        splatted[96 * c : 96 * c + 32] + splatted[96 * c + 32 : 96 * c + 64] + splatted[96 * c + 64 : 96 * c + 96]
        for c in range(3)
    ]
    shifted_diagonal = 16.5 + 2.0 * splatted[288:320]

    def halo(source, turn, begin):
        for a, b in offsets:
            place = (a + 1) * 3 + b + 1

            @pl.when(inside(a, b))
            def _(a=a, b=b, place=place):
                if begin:
                    pltpu.make_async_remote_copy(
                        src_ref=source.at[pl.ds(8, 2)],
                        dst_ref=source.at[pl.ds(2 * (8 - place), 2)],
                        send_sem=halo_send.at[turn, place],
                        recv_sem=halo_recv.at[turn, 8 - place],
                        device_id=(wide + a, narrow + b),
                        device_id_type=MESH,
                    ).start()
                else:
                    got = source.at[pl.ds(2 * place, 2)]
                    pltpu.make_async_copy(got, got, halo_recv.at[turn, place]).wait()

    def near(brick, a, b, c):
        return near_ref[0, 0, brick, (a + 1) * 9 + (b + 1) * 3 + c + 1]

    y_at, z_at = lanes(16)
    row_at = lax.broadcasted_iota(jnp.int32, (16, 256), 0)

    for brick in range(2):
        for c in range(3):
            vector_src[8 + brick, c] = vectors[c][16 * brick : 16 * brick + 16]
    halo(vector_src, 0, True)
    halo(vector_src, 0, False)
    sides = []
    for brick in range(2):
        own = [vectors[c][16 * brick : 16 * brick + 16] for c in range(3)]
        low = vector_src[near(brick, -1, 0, 0), 0, 15:16, :]
        high = vector_src[near(brick, 1, 0, 0), 0, 0:1, :]
        change = jnp.where(row_at == 15, high, pltpu.roll(own[0], 15, 0)) - jnp.where(
            row_at == 0, low, pltpu.roll(own[0], 1, 0)
        )
        low = vector_src[near(brick, 0, -1, 0), 1]
        high = vector_src[near(brick, 0, 1, 0), 1]
        change = change + (
            pltpu.roll(jnp.where(y_at == 0, high, own[1]), 240, 1)
            - pltpu.roll(jnp.where(y_at == 15, low, own[1]), 16, 1)
        )
        low = vector_src[near(brick, 0, 0, -1), 2]
        high = vector_src[near(brick, 0, 0, 1), 2]
        change = change + (
            jnp.where(z_at == 15, pltpu.roll(high, 15, 1), pltpu.roll(own[2], 255, 1))
            - jnp.where(z_at == 0, pltpu.roll(low, 241, 1), pltpu.roll(own[2], 1, 1))
        )
        sides.append(-4.0 * change)
    residual = jnp.concatenate(sides, 0)

    def send_field(turn, values):
        for brick in range(2):
            field_src[turn][8 + brick] = values[16 * brick : 16 * brick + 16]
        halo(field_src[turn], 1 + turn, True)

    def operator(turn, values):
        halo(field_src[turn], 1 + turn, False)
        images = []
        for brick in range(2):
            columns = []
            for b in (-1, 0, 1):
                pieces = []
                for c in (-1, 0, 1):
                    if b == 0 and c == 0:
                        here = values[16 * brick : 16 * brick + 16]
                    else:
                        here = field_src[turn][near(brick, 0, b, c)]
                    low = field_src[turn][near(brick, -1, b, c), 15:16, :]
                    high = field_src[turn][near(brick, 1, b, c), 0:1, :]
                    pieces.append(
                        here
                        + 0.5
                        * (
                            jnp.where(row_at == 0, low, pltpu.roll(here, 1, 0))
                            + jnp.where(row_at == 15, high, pltpu.roll(here, 15, 0))
                        )
                    )
                columns.append(
                    pieces[1]
                    + 0.5
                    * (
                        jnp.where(z_at == 0, pltpu.roll(pieces[0], 241, 1), pltpu.roll(pieces[1], 1, 1))
                        + jnp.where(z_at == 15, pltpu.roll(pieces[2], 15, 1), pltpu.roll(pieces[1], 255, 1))
                    )
                )
            images.append(
                columns[1]
                + 0.5
                * (
                    pltpu.roll(jnp.where(y_at == 15, columns[0], columns[1]), 16, 1)
                    + pltpu.roll(jnp.where(y_at == 0, columns[2], columns[1]), 240, 1)
                )
            )
        return shifted_diagonal * values - 2.0 * jnp.concatenate(images, 0)

    def send_sums(turn, one, two):
        for row, values in enumerate((one, two)):
            summed = jnp.sum(values, axis=0, keepdims=True)
            part_out[turn, row : row + 1] = summed[:, :128] + summed[:, 128:]
        part_in[turn, pl.ds(me, 1)] = part_out[pl.ds(turn, 1)]

        @pl.loop(1, devices)
        def _(k):
            other = lax.rem(me + k, devices)
            pltpu.make_async_remote_copy(
                src_ref=part_out.at[turn],
                dst_ref=part_in.at[turn, me],
                send_sem=part_send.at[turn],
                recv_sem=part_recv.at[turn],
                device_id=(other // narrows, lax.rem(other, narrows)),
                device_id_type=MESH,
            ).start()

    def get_sums(turn):
        got = part_in.at[turn, pl.ds(0, devices - 1)]
        pltpu.make_async_copy(got, got, part_recv.at[turn]).wait()
        total = jnp.sum(jnp.sum(part_in[turn], axis=0), axis=1, keepdims=True)
        return total[0:1], total[1:2]

    send_field(0, residual)
    image = operator(0, residual)

    send_field(1, image)
    send_sums(0, residual * residual, residual * image)
    second = operator(1, image)
    square_0, product = get_sums(0)
    step_0 = square_0 / product
    answer = step_0 * residual
    towards, towards_image, towards_second = residual, image, second
    residual = residual - step_0 * image
    image = image - step_0 * second

    send_field(2, image)
    send_sums(1, residual * residual, residual * image)
    second = operator(2, image)
    square_1, product = get_sums(1)
    ratio = square_1 / square_0
    step_1 = square_1 / (product - ratio * square_1 / step_0)
    towards = residual + ratio * towards
    towards_image = image + ratio * towards_image
    towards_second = second + ratio * towards_second
    answer = answer + step_1 * towards
    residual = residual - step_1 * towards_image
    image = image - step_1 * towards_second

    send_sums(2, residual * residual, residual * image)
    square_2, product = get_sums(2)
    ratio = square_2 / square_1
    step_2 = square_2 / (product - ratio * square_2 / step_1)
    towards = residual + ratio * towards
    towards_image = image + ratio * towards_image
    answer = answer + step_2 * towards
    residual = residual - step_2 * towards_image

    for brick in range(2):
        for x in range(16):
            at = (0, 0, slice(brick, brick + 1), slice(256 * x, 256 * x + 256))
            solution_ref[at] = answer[16 * brick + x : 16 * brick + x + 1]
            residual_ref[at] = residual[16 * brick + x : 16 * brick + x + 1]

    sent = point_out.at[pl.ds(0, wides - 1)]
    pltpu.make_async_copy(sent, sent, point_send.at[0]).wait()
    for turn in range(3):
        sent = part_in.at[turn, pl.ds(0, devices - 1)]
        pltpu.make_async_copy(sent, sent, part_send.at[turn]).wait()
    for a, b in offsets:
        place = (a + 1) * 3 + b + 1

        @pl.when(inside(a, b))
        def _(place=place):
            sent = vector_src.at[pl.ds(8, 2)]
            pltpu.make_async_copy(sent, sent, halo_send.at[0, place]).wait()
            for turn in range(3):
                sent = field_src[turn].at[pl.ds(8, 2)]
                pltpu.make_async_copy(sent, sent, halo_send.at[1 + turn, place]).wait()


def shards(wides, narrows, point_owner, point_cell, normals, strip_count, neighbours):
    points = point_cell.shape[0]
    devices = wides * narrows
    slots = 2 * points // wides
    vmem = pl.BlockSpec(memory_space=pltpu.VMEM)
    smem = pl.BlockSpec(memory_space=pltpu.SMEM)
    out = jax.ShapeDtypeStruct((1, 1, 2, 4096), F32)
    return pl.pallas_call(
        functools.partial(kernel, wides, narrows),
        out_shape=(out, out),
        in_specs=[vmem, vmem, vmem, smem, smem],
        out_specs=(vmem, vmem),
        scratch_shapes=[
            pltpu.VMEM((8, points), F32),
            pltpu.VMEM((wides, 8, slots), F32),
            pltpu.VMEM((wides, 8, slots), F32),
            pltpu.VMEM((19, 3, 16, 256), F32),
            pltpu.VMEM((19, 16, 256), F32),
            pltpu.VMEM((19, 16, 256), F32),
            pltpu.VMEM((19, 16, 256), F32),
            pltpu.VMEM((3, 2, 128), F32),
            pltpu.VMEM((3, devices, 2, 128), F32),
            pltpu.SemaphoreType.DMA((1,)),
            pltpu.SemaphoreType.DMA((1,)),
            pltpu.SemaphoreType.DMA((4, 9)),
            pltpu.SemaphoreType.DMA((4, 9)),
            pltpu.SemaphoreType.DMA((3,)),
            pltpu.SemaphoreType.DMA((3,)),
        ],
        compiler_params=pltpu.CompilerParams(
            collective_id=0, has_side_effects=True, vmem_limit_bytes=32 * 1024 * 1024
        ),
    )(
        point_owner.reshape(1, points), point_cell.reshape(1, points), normals, strip_count, neighbours
    )


def solution(mesh):
    return jax.shard_map(
        functools.partial(shards, mesh.shape["wide"], mesh.shape["narrow"]),
        mesh=mesh,
        in_specs=(
            P(("wide", "narrow"), None),
            P(("wide", "narrow")),
            P(None, ("wide", "narrow")),
            P(("wide", "narrow")),
            P("wide", "narrow", None, None),
        ),
        out_specs=(P("wide", "narrow", None, None), P("wide", "narrow", None, None)),
        check_vma=False,
    )
```

```python
import functools

import jax
import jax.numpy as jnp
from jax import lax
from jax.experimental import pallas as pl
from jax.experimental.pallas import tpu as pltpu
from jax.sharding import PartitionSpec as P

MESH = pl.DeviceIdType.MESH
NT = (((1,), (1,)), ((), ()))
F32 = jnp.float32
BF16 = jnp.bfloat16


def split3(values):
    high = values.astype(BF16).astype(F32)
    rest = values - high
    middle = rest.astype(BF16).astype(F32)
    return high, middle, rest - middle


def one_if(condition):
    return jnp.where(condition, 1.0, 0.0)


def edge(offset):
    return one_if(offset == 0) + 0.5 * one_if((offset == 1) | (offset == -1))


def pack_matrix():
    cell = lax.broadcasted_iota(jnp.int32, (256, 128), 0)
    lane = lax.broadcasted_iota(jnp.int32, (256, 128), 1)
    side, k = (lane // 16) % 4, lane % 16
    wanted = jnp.where(side < 2, k + 240 * side, 16 * k + 15 * (side - 2))
    return one_if(cell == wanted).astype(BF16)


def halo_matrices():
    lane = lax.broadcasted_iota(jnp.int32, (128, 256), 0)
    cell = lax.broadcasted_iota(jnp.int32, (128, 256), 1)
    y, z = cell // 16, cell % 16
    side, k = lane // 16, lane % 16
    face_y = (one_if(side == 0) * one_if(y == 15), one_if(side == 1) * one_if(y == 0))
    face_z = (one_if(side == 2) * one_if(z == 15), one_if(side == 3) * one_if(z == 0))
    corner = (
        one_if((lane == 64) & (y == 15) & (z == 15))
        + one_if((lane == 79) & (y == 15) & (z == 0))
        + one_if((lane == 80) & (y == 0) & (z == 15))
        + one_if((lane == 95) & (y == 0) & (z == 0))
    )
    weight = 0.5 * ((face_y[0] + face_y[1]) * edge(z - k) + (face_z[0] + face_z[1]) * edge(y - k)) + 0.25 * corner
    slope = (face_y[0] - face_y[1]) * one_if(z == k) + (face_z[0] - face_z[1]) * one_if(y == k)
    return weight.astype(BF16), slope.astype(BF16)


def exact_dot(values, matrix):
    rows = values.shape[0]
    parts = jnp.concatenate(split3(values), 0).astype(BF16)
    summed = jnp.dot(parts, matrix, preferred_element_type=F32)
    return summed[:rows] + summed[rows : 2 * rows] + summed[2 * rows :]


def kernel(
    wides, narrows, owner_hbm, cell_hbm, normal_hbm, count_ref, near_ref, solution_ref, residual_ref,
    owner_ref, cell_ref, normal_ref, pack_ref, weight_ref, slope_ref,
    point_rows, point_out, point_in, vector_src, field_0, field_1, field_2, part_out, part_in,
    in_sem, point_send, point_recv, halo_send, halo_recv, part_send, part_recv,
):
    devices = wides * narrows
    wide = lax.axis_index("wide")
    narrow = lax.axis_index("narrow")
    me = wide * narrows + narrow
    points = cell_ref.shape[1]
    slots = point_out.shape[2]
    loads = [
        pltpu.make_async_copy(source, target, in_sem.at[k])
        for k, (source, target) in enumerate(
            ((owner_hbm, owner_ref), (cell_hbm, cell_ref), (normal_hbm, normal_ref))
        )
    ]
    for load in loads:
        load.start()
    barrier = pltpu.get_barrier_semaphore()

    @pl.loop(1, devices)
    def _(k):
        other = lax.rem(me + k, devices)
        pl.semaphore_signal(
            barrier, inc=1, device_id=(other // narrows, lax.rem(other, narrows)), device_id_type=MESH
        )

    offsets = [(a, b) for a in (-1, 0, 1) for b in (-1, 0, 1) if (a, b) != (0, 0)]

    def inside(a, b):
        return (wide + a >= 0) & (wide + a < wides) & (narrow + b >= 0) & (narrow + b < narrows)

    sources = (vector_src, field_0, field_1, field_2)
    for source in sources:
        source[18] = jnp.zeros((12, 128), F32)
    for a, b in offsets:
        place = (a + 1) * 3 + b + 1

        @pl.when(jnp.logical_not(inside(a, b)))
        def _(place=place):
            for source in sources:
                source[2 * place : 2 * place + 2] = jnp.zeros((2, 12, 128), F32)

    for load in loads:
        load.wait()

    owner = owner_ref[...]
    live = lax.broadcasted_iota(jnp.int32, (1, points), 1) < count_ref[0]
    owner_hot = jnp.where(
        lax.broadcasted_iota(jnp.int32, (wides, points), 0) == owner, 1.0, 0.0
    )
    blocks = points // 128
    stacked = jnp.concatenate([owner_hot[:, k * 128 : (k + 1) * 128] for k in range(blocks)], 0)
    earlier = jnp.where(
        lax.broadcasted_iota(jnp.int32, (128, 256), 0) < lax.broadcasted_iota(jnp.int32, (128, 256), 1),
        1.0,
        0.0,
    )
    counted = jnp.dot(stacked.astype(BF16), earlier.astype(BF16), preferred_element_type=F32)
    ranks = []
    before = jnp.zeros((wides, 128), F32)
    for k in range(blocks):
        rows = slice(k * wides, (k + 1) * wides)
        ranks.append(
            jnp.sum(stacked[rows] * (counted[rows, :128] + before), axis=0, keepdims=True)
        )
        before = before + counted[rows, 128:]
    slot = jnp.concatenate(ranks, 1).astype(jnp.int32) + owner * slots

    point_rows[0:3] = normal_ref[...]
    point_rows[3:4] = jnp.where(live, cell_ref[...] + 1, 0).astype(F32)
    point_rows[4:8] = jnp.zeros((4, points), F32)
    split_rows = jnp.concatenate(
        split3(point_rows[...]) + (jnp.zeros((8, points), F32),), 0
    ).astype(BF16)
    joined = 2 if slots % 128 == 0 and wides % 2 == 0 else 1
    slot_row = lax.broadcasted_iota(jnp.int32, (joined * slots, points), 0)
    for k in range(0, wides, joined):
        hot = jnp.where(slot_row == slot - k * slots, 1.0, 0.0).astype(BF16)
        moved = lax.dot_general(split_rows, hot, NT, preferred_element_type=F32)
        moved = moved[0:8] + moved[8:16] + moved[16:24]
        for j in range(joined):
            point_out[k + j] = moved[:, j * slots : (j + 1) * slots]

    pl.semaphore_wait(barrier, devices - 1)

    @pl.loop(1, wides)
    def _(k):
        other = lax.rem(wide + k, wides)
        pltpu.make_async_remote_copy(
            src_ref=point_out.at[other],
            dst_ref=point_in.at[wide],
            send_sem=point_send.at[0],
            recv_sem=point_recv.at[0],
            device_id=(other, narrow),
            device_id_type=MESH,
        ).start()

    pack_ref[...] = pack_matrix()
    weight_ref[...], slope_ref[...] = halo_matrices()
    point_in[pl.ds(wide, 1)] = point_out[pl.ds(wide, 1)]
    arrived = point_in.at[pl.ds(0, wides - 1)]
    pltpu.make_async_copy(arrived, arrived, point_recv.at[0]).wait()

    group = 8 if slots % 128 == 0 and wides % 8 == 0 else 1
    splatted = jnp.zeros((320, 256), F32)
    for k in range(0, wides, group):
        got = jnp.concatenate([point_in[k + j] for j in range(group)], 1)
        width = group * slots
        cell = got[3:4].astype(jnp.int32) - 1
        row_hot = lax.broadcasted_iota(jnp.int32, (32, width), 0) == lax.shift_right_arithmetic(cell, 8)
        lane_hot = lax.broadcasted_iota(jnp.int32, (256, width), 0) == (cell & 255)
        weights = []
        for c in range(3):
            weights.extend(split3(got[c : c + 1]))
        weights.append(jnp.ones((1, width), F32))
        weighted = jnp.concatenate([jnp.where(row_hot, w, 0.0) for w in weights], 0).astype(BF16)
        splatted = splatted + lax.dot_general(
            weighted, jnp.where(lane_hot, 1.0, 0.0).astype(BF16), NT, preferred_element_type=F32
        )
    vectors = [
        splatted[96 * c : 96 * c + 32] + splatted[96 * c + 32 : 96 * c + 64] + splatted[96 * c + 64 : 96 * c + 96]
        for c in range(3)
    ]
    shifted_diagonal = 16.5 + 2.0 * splatted[288:320]

    def halo(source, turn, begin):
        for a, b in offsets:
            place = (a + 1) * 3 + b + 1

            @pl.when(inside(a, b))
            def _(a=a, b=b, place=place):
                if begin:
                    pltpu.make_async_remote_copy(
                        src_ref=source.at[pl.ds(8, 2)],
                        dst_ref=source.at[pl.ds(2 * (8 - place), 2)],
                        send_sem=halo_send.at[turn, place],
                        recv_sem=halo_recv.at[turn, 8 - place],
                        device_id=(wide + a, narrow + b),
                        device_id_type=MESH,
                    ).start()
                else:
                    got = source.at[pl.ds(2 * place, 2)]
                    pltpu.make_async_copy(got, got, halo_recv.at[turn, place]).wait()

    def near(brick, a, b, c):
        return near_ref[0, 0, brick, (a + 1) * 9 + (b + 1) * 3 + c + 1]

    cell_at = lax.broadcasted_iota(jnp.int32, (32, 256), 1)
    x_at = lax.broadcasted_iota(jnp.int32, (32, 256), 0) % 16
    y_at, z_at = cell_at // 16, cell_at % 16
    low_half = lax.broadcasted_iota(jnp.int32, (8, 128), 1) < 64

    def send_faces(turn, ends, packed):
        source = sources[turn]
        for brick in range(2):
            row = 16 * brick
            source[8 + brick, 0:8] = jnp.where(low_half, packed[row : row + 8], packed[row + 8 : row + 16])
            for k, x in enumerate((0, 15)):
                for half in range(2):
                    at = 8 + 2 * k + half
                    source[8 + brick, at : at + 1] = ends[row + x : row + x + 1, 128 * half : 128 * half + 128]
        halo(source, turn, True)

    def ends_of(source):
        rows = []
        for brick in range(2):
            low, high = near(brick, -1, 0, 0), near(brick, 1, 0, 0)
            low = jnp.concatenate([source[low, 10:11, :], source[low, 11:12, :]], 1)
            high = jnp.concatenate([source[high, 8:9, :], source[high, 9:10, :]], 1)
            rows.append((low, high))
        low = jnp.concatenate([jnp.broadcast_to(rows[brick][0], (16, 256)) for brick in range(2)], 0)
        high = jnp.concatenate([jnp.broadcast_to(rows[brick][1], (16, 256)) for brick in range(2)], 0)
        return low, high

    def merged(source, brick, a, rows, corners):
        lane = lax.broadcasted_iota(jnp.int32, (rows.stop - rows.start, 128), 1) % 64

        def beside(b, c):
            return source[near(brick, a, b, c), rows, :]

        faces = jnp.where(
            lane < 32,
            jnp.where(lane < 16, beside(1, 0), beside(-1, 0)),
            jnp.where(lane < 48, beside(0, 1), beside(0, -1)),
        )
        if not corners:
            return faces, faces
        corner = jnp.where(
            lane < 16,
            jnp.where(lane == 0, beside(1, 1), beside(1, -1)),
            jnp.where(lane == 16, beside(-1, 1), beside(-1, -1)),
        )
        return faces, corner

    def swap(values):
        return pltpu.roll(values, 64, 1)

    def faces_of(source, brick, corners):
        faces, corner = merged(source, brick, 0, slice(0, 8), corners)
        return jnp.concatenate(
            [jnp.where(low_half, faces, swap(corner)), jnp.where(low_half, swap(faces), corner)], 0
        )

    send_faces(
        0,
        vectors[0],
        jnp.where(
            lax.broadcasted_iota(jnp.int32, (32, 128), 1) % 64 < 32,
            exact_dot(vectors[1], pack_ref[...]),
            exact_dot(vectors[2], pack_ref[...]),
        ),
    )
    change = (
        jnp.where(x_at == 15, 0.0, pltpu.roll(vectors[0], 31, 0))
        - jnp.where(x_at == 0, 0.0, pltpu.roll(vectors[0], 1, 0))
        + jnp.where(y_at == 15, 0.0, pltpu.roll(vectors[1], 240, 1))
        - jnp.where(y_at == 0, 0.0, pltpu.roll(vectors[1], 16, 1))
        + jnp.where(z_at == 15, 0.0, pltpu.roll(vectors[2], 255, 1))
        - jnp.where(z_at == 0, 0.0, pltpu.roll(vectors[2], 1, 1))
    )
    halo(vector_src, 0, False)
    low, high = ends_of(vector_src)
    faces = jnp.concatenate([faces_of(vector_src, brick, False) for brick in range(2)], 0)
    change = (
        change
        + jnp.where(x_at == 15, high, 0.0)
        - jnp.where(x_at == 0, low, 0.0)
        + exact_dot(faces, slope_ref[...])
    )
    residual = -4.0 * change

    def send_field(turn, values):
        send_faces(1 + turn, values, exact_dot(values, pack_ref[...]))

    def plane_sum(values):
        summed = values + 0.5 * (
            jnp.where(z_at == 0, 0.0, pltpu.roll(values, 1, 1))
            + jnp.where(z_at == 15, 0.0, pltpu.roll(values, 255, 1))
        )
        return summed + 0.5 * (
            jnp.where(y_at == 0, 0.0, pltpu.roll(summed, 16, 1))
            + jnp.where(y_at == 15, 0.0, pltpu.roll(summed, 240, 1))
        )

    def operator(turn, values):
        source = sources[1 + turn]
        inner = values + 0.5 * (
            jnp.where(x_at == 0, 0.0, pltpu.roll(values, 1, 0))
            + jnp.where(x_at == 15, 0.0, pltpu.roll(values, 31, 0))
        )
        own = shifted_diagonal * values - 2.0 * plane_sum(inner)
        halo(source, 1 + turn, False)
        low, high = ends_of(source)
        ends = plane_sum(jnp.where(x_at == 0, low, jnp.where(x_at == 15, high, 0.0)))
        row_at = lax.broadcasted_iota(jnp.int32, (16, 128), 0)
        half_row = lax.broadcasted_iota(jnp.int32, (1, 128), 1) < 64
        faces = []
        for brick in range(2):
            here = faces_of(source, brick, True)
            face, corner = merged(source, brick, -1, slice(7, 8), True)
            low = jnp.where(half_row, swap(face), corner)
            face, corner = merged(source, brick, 1, slice(0, 1), True)
            high = jnp.where(half_row, face, swap(corner))
            faces.append(
                here
                + 0.5
                * (
                    jnp.where(row_at == 0, low, pltpu.roll(here, 1, 0))
                    + jnp.where(row_at == 15, high, pltpu.roll(here, 15, 0))
                )
            )
        return own - ends - 2.0 * exact_dot(jnp.concatenate(faces, 0), weight_ref[...])

    def send_sums(turn, one, two):
        for row, values in enumerate((one, two)):
            summed = jnp.sum(values, axis=0, keepdims=True)
            part_out[turn, row : row + 1] = summed[:, :128] + summed[:, 128:]
        part_in[turn, pl.ds(me, 1)] = part_out[pl.ds(turn, 1)]

        @pl.loop(1, devices)
        def _(k):
            other = lax.rem(me + k, devices)
            pltpu.make_async_remote_copy(
                src_ref=part_out.at[turn],
                dst_ref=part_in.at[turn, me],
                send_sem=part_send.at[turn],
                recv_sem=part_recv.at[turn],
                device_id=(other // narrows, lax.rem(other, narrows)),
                device_id_type=MESH,
            ).start()

    def get_sums(turn):
        got = part_in.at[turn, pl.ds(0, devices - 1)]
        pltpu.make_async_copy(got, got, part_recv.at[turn]).wait()
        total = jnp.sum(jnp.sum(part_in[turn], axis=0), axis=1, keepdims=True)
        return total[0:1], total[1:2]

    send_field(0, residual)
    image = operator(0, residual)

    send_field(1, image)
    send_sums(0, residual * residual, residual * image)
    second = operator(1, image)
    square_0, product = get_sums(0)
    step_0 = square_0 / product
    answer = step_0 * residual
    towards, towards_image, towards_second = residual, image, second
    residual = residual - step_0 * image
    image = image - step_0 * second

    send_field(2, image)
    send_sums(1, residual * residual, residual * image)
    second = operator(2, image)
    square_1, product = get_sums(1)
    ratio = square_1 / square_0
    step_1 = square_1 / (product - ratio * square_1 / step_0)
    towards = residual + ratio * towards
    towards_image = image + ratio * towards_image
    towards_second = second + ratio * towards_second
    answer = answer + step_1 * towards
    residual = residual - step_1 * towards_image
    image = image - step_1 * towards_second

    send_sums(2, residual * residual, residual * image)
    square_2, product = get_sums(2)
    ratio = square_2 / square_1
    step_2 = square_2 / (product - ratio * square_2 / step_1)
    towards = residual + ratio * towards
    towards_image = image + ratio * towards_image
    answer = answer + step_2 * towards
    residual = residual - step_2 * towards_image

    for brick in range(2):
        for x in range(16):
            at = (0, 0, slice(brick, brick + 1), slice(256 * x, 256 * x + 256))
            solution_ref[at] = answer[16 * brick + x : 16 * brick + x + 1]
            residual_ref[at] = residual[16 * brick + x : 16 * brick + x + 1]

    sent = point_out.at[pl.ds(0, wides - 1)]
    pltpu.make_async_copy(sent, sent, point_send.at[0]).wait()
    for turn in range(3):
        sent = part_in.at[turn, pl.ds(0, devices - 1)]
        pltpu.make_async_copy(sent, sent, part_send.at[turn]).wait()
    for a, b in offsets:
        place = (a + 1) * 3 + b + 1

        @pl.when(inside(a, b))
        def _(place=place):
            for turn, source in enumerate(sources):
                sent = source.at[pl.ds(8, 2)]
                pltpu.make_async_copy(sent, sent, halo_send.at[turn, place]).wait()


def shards(wides, narrows, point_owner, point_cell, normals, strip_count, neighbours):
    points = point_cell.shape[0]
    devices = wides * narrows
    slots = 2 * points // wides
    vmem = pl.BlockSpec(memory_space=pltpu.VMEM)
    hbm = pl.BlockSpec(memory_space=pltpu.HBM)
    smem = pl.BlockSpec(memory_space=pltpu.SMEM)
    out = jax.ShapeDtypeStruct((1, 1, 2, 4096), F32)
    return pl.pallas_call(
        functools.partial(kernel, wides, narrows),
        out_shape=(out, out),
        in_specs=[hbm, hbm, hbm, smem, smem],
        out_specs=(vmem, vmem),
        scratch_shapes=[
            pltpu.VMEM((1, points), jnp.int32),
            pltpu.VMEM((1, points), jnp.int32),
            pltpu.VMEM((3, points), F32),
            pltpu.VMEM((256, 128), BF16),
            pltpu.VMEM((128, 256), BF16),
            pltpu.VMEM((128, 256), BF16),
            pltpu.VMEM((8, points), F32),
            pltpu.VMEM((wides, 8, slots), F32),
            pltpu.VMEM((wides, 8, slots), F32),
            pltpu.VMEM((19, 12, 128), F32),
            pltpu.VMEM((19, 12, 128), F32),
            pltpu.VMEM((19, 12, 128), F32),
            pltpu.VMEM((19, 12, 128), F32),
            pltpu.VMEM((3, 2, 128), F32),
            pltpu.VMEM((3, devices, 2, 128), F32),
            pltpu.SemaphoreType.DMA((3,)),
            pltpu.SemaphoreType.DMA((1,)),
            pltpu.SemaphoreType.DMA((1,)),
            pltpu.SemaphoreType.DMA((4, 9)),
            pltpu.SemaphoreType.DMA((4, 9)),
            pltpu.SemaphoreType.DMA((3,)),
            pltpu.SemaphoreType.DMA((3,)),
        ],
        compiler_params=pltpu.CompilerParams(
            collective_id=0, has_side_effects=True, vmem_limit_bytes=32 * 1024 * 1024
        ),
    )(
        point_owner.reshape(1, points), point_cell.reshape(1, points), normals, strip_count, neighbours
    )


def solution(mesh):
    return jax.shard_map(
        functools.partial(shards, mesh.shape["wide"], mesh.shape["narrow"]),
        mesh=mesh,
        in_specs=(
            P(("wide", "narrow"), None),
            P(("wide", "narrow")),
            P(None, ("wide", "narrow")),
            P(("wide", "narrow")),
            P("wide", "narrow", None, None),
        ),
        out_specs=(P("wide", "narrow", None, None), P("wide", "narrow", None, None)),
        check_vma=False,
    )
```

```python
import functools

import jax
import jax.numpy as jnp
from jax import lax
from jax.experimental import pallas as pl
from jax.experimental.pallas import tpu as pltpu
from jax.sharding import PartitionSpec as P

MESH = pl.DeviceIdType.MESH
NT = (((1,), (1,)), ((), ()))
F32 = jnp.float32
BF16 = jnp.bfloat16


def split3(values):
    high = values.astype(BF16).astype(F32)
    rest = values - high
    middle = rest.astype(BF16).astype(F32)
    return high, middle, rest - middle


def one_if(condition):
    return jnp.where(condition, 1.0, 0.0)


def edge(offset):
    return one_if(offset == 0) + 0.5 * one_if((offset == 1) | (offset == -1))


def pack_matrix():
    cell = lax.broadcasted_iota(jnp.int32, (256, 128), 0)
    lane = lax.broadcasted_iota(jnp.int32, (256, 128), 1)
    side, k = (lane // 16) % 4, lane % 16
    wanted = jnp.where(side < 2, k + 240 * side, 16 * k + 15 * (side - 2))
    return one_if(cell == wanted).astype(BF16)


def halo_matrices():
    lane = lax.broadcasted_iota(jnp.int32, (128, 256), 0)
    cell = lax.broadcasted_iota(jnp.int32, (128, 256), 1)
    y, z = cell // 16, cell % 16
    side, k = lane // 16, lane % 16
    face_y = (one_if(side == 0) * one_if(y == 15), one_if(side == 1) * one_if(y == 0))
    face_z = (one_if(side == 2) * one_if(z == 15), one_if(side == 3) * one_if(z == 0))
    corner = (
        one_if((lane == 64) & (y == 15) & (z == 15))
        + one_if((lane == 79) & (y == 15) & (z == 0))
        + one_if((lane == 80) & (y == 0) & (z == 15))
        + one_if((lane == 95) & (y == 0) & (z == 0))
    )
    weight = 0.5 * ((face_y[0] + face_y[1]) * edge(z - k) + (face_z[0] + face_z[1]) * edge(y - k)) + 0.25 * corner
    slope = (face_y[0] - face_y[1]) * one_if(z == k) + (face_z[0] - face_z[1]) * one_if(y == k)
    return weight.astype(BF16), slope.astype(BF16)


def exact_dot(values, matrix):
    rows = values.shape[0]
    parts = jnp.concatenate(split3(values), 0).astype(BF16)
    summed = jnp.dot(parts, matrix, preferred_element_type=F32)
    return summed[:rows] + summed[rows : 2 * rows] + summed[2 * rows :]


def kernel(
    wides, narrows, owner_hbm, cell_hbm, normal_hbm, count_ref, near_ref, solution_ref, residual_ref,
    owner_ref, cell_ref, normal_ref, pack_ref, weight_ref, slope_ref,
    point_out, point_in, vector_src, field_0, field_1, field_2, part_out, part_in,
    in_sem, point_send, point_recv, halo_send, halo_recv, part_send, part_recv,
):
    devices = wides * narrows
    wide = lax.axis_index("wide")
    narrow = lax.axis_index("narrow")
    me = wide * narrows + narrow
    points = cell_ref.shape[1]
    slots = point_out.shape[2]
    loads = [
        pltpu.make_async_copy(source, target, in_sem.at[k])
        for k, (source, target) in enumerate(
            ((owner_hbm, owner_ref), (cell_hbm, cell_ref), (normal_hbm, normal_ref))
        )
    ]
    for load in loads:
        load.start()
    barrier = pltpu.get_barrier_semaphore()

    def after(at, step, count):
        return jnp.where(at + step >= count, at + step - count, at + step)

    def each_device(act):
        if devices > 64:

            @pl.loop(1, devices)
            def _(k):
                other = lax.rem(me + k, devices)
                act((other // narrows, lax.rem(other, narrows)))

            return
        for step in range(1, devices):
            act((wide_after[step // narrows], narrow_after[step % narrows]))

    wide_after = [wide] + [after(wide, k, wides) for k in range(1, wides)]
    narrow_after = [narrow] + [after(narrow, k, narrows) for k in range(1, narrows)]
    each_device(lambda to: pl.semaphore_signal(barrier, inc=1, device_id=to, device_id_type=MESH))

    offsets = [(a, b) for a in (-1, 0, 1) for b in (-1, 0, 1) if (a, b) != (0, 0)]

    def inside(a, b):
        return (wide + a >= 0) & (wide + a < wides) & (narrow + b >= 0) & (narrow + b < narrows)

    sources = (vector_src, field_0, field_1, field_2)
    for source in sources:
        source[18] = jnp.zeros((12, 128), F32)
    for a, b in offsets:
        place = (a + 1) * 3 + b + 1

        @pl.when(jnp.logical_not(inside(a, b)))
        def _(place=place):
            for source in sources:
                source[2 * place : 2 * place + 2] = jnp.zeros((2, 12, 128), F32)

    for load in loads:
        load.wait()

    owner = owner_ref[...]
    live = lax.broadcasted_iota(jnp.int32, (1, points), 1) < count_ref[0]
    owned = lax.broadcasted_iota(jnp.int32, (wides, points), 0) == owner
    owner_hot = one_if(owned)
    blocks = points // 128
    stacked = jnp.concatenate([owner_hot[:, k * 128 : (k + 1) * 128] for k in range(blocks)], 0)
    earlier = jnp.where(
        lax.broadcasted_iota(jnp.int32, (128, 256), 0) < lax.broadcasted_iota(jnp.int32, (128, 256), 1),
        1.0,
        0.0,
    )
    counted = jnp.dot(stacked.astype(BF16), earlier.astype(BF16), preferred_element_type=F32)
    ranks = []
    before = jnp.zeros((wides, 128), F32)
    for k in range(blocks):
        rows = slice(k * wides, (k + 1) * wides)
        ranks.append(
            jnp.sum(stacked[rows] * (counted[rows, :128] + before), axis=0, keepdims=True)
        )
        before = before + counted[rows, 128:]
    rank = jnp.concatenate(ranks, 1).astype(jnp.int32)
    code = jnp.where(live, cell_ref[...] + 1, 0)
    rows = [lax.shift_right_logical(code, 8).astype(F32), (code & 255).astype(F32)]
    for c in range(3):
        rows.extend(split3(normal_ref[c : c + 1]))
    weighted = jnp.concatenate([jnp.where(owned, row, 0.0) for row in rows], 0).astype(BF16)
    rank_hot = one_if(lax.broadcasted_iota(jnp.int32, (slots, points), 0) == rank).astype(BF16)
    moved = lax.dot_general(weighted, rank_hot, NT, preferred_element_type=F32)
    moved = [moved[k * wides : (k + 1) * wides] for k in range(11)]
    values = [moved[2 + 3 * c] + moved[3 + 3 * c] + moved[4 + 3 * c] for c in range(3)]
    values.append(256.0 * moved[0] + moved[1])
    for k in range(wides):
        for c in range(4):
            point_out[k, c : c + 1] = values[c][k : k + 1]

    pl.semaphore_wait(barrier, devices - 1)

    for other in wide_after[1:]:
        pltpu.make_async_remote_copy(
            src_ref=point_out.at[other],
            dst_ref=point_in.at[wide],
            send_sem=point_send.at[0],
            recv_sem=point_recv.at[0],
            device_id=(other, narrow),
            device_id_type=MESH,
        ).start()

    pack_ref[...] = pack_matrix()
    weight_ref[...], slope_ref[...] = halo_matrices()
    point_in[pl.ds(wide, 1)] = point_out[pl.ds(wide, 1)]
    arrived = point_in.at[pl.ds(0, wides - 1)]
    pltpu.make_async_copy(arrived, arrived, point_recv.at[0]).wait()

    group = 8 if slots % 128 == 0 and wides % 8 == 0 else 1
    splatted = jnp.zeros((320, 256), F32)
    for k in range(0, wides, group):
        got = jnp.concatenate([point_in[k + j] for j in range(group)], 1)
        width = group * slots
        cell = got[3:4].astype(jnp.int32) - 1
        row_hot = lax.broadcasted_iota(jnp.int32, (32, width), 0) == lax.shift_right_arithmetic(cell, 8)
        lane_hot = lax.broadcasted_iota(jnp.int32, (256, width), 0) == (cell & 255)
        weights = []
        for c in range(3):
            weights.extend(split3(got[c : c + 1]))
        weights.append(jnp.ones((1, width), F32))
        weighted = jnp.concatenate([jnp.where(row_hot, w, 0.0) for w in weights], 0).astype(BF16)
        splatted = splatted + lax.dot_general(
            weighted, jnp.where(lane_hot, 1.0, 0.0).astype(BF16), NT, preferred_element_type=F32
        )
    vectors = [
        splatted[96 * c : 96 * c + 32] + splatted[96 * c + 32 : 96 * c + 64] + splatted[96 * c + 64 : 96 * c + 96]
        for c in range(3)
    ]
    shifted_diagonal = 16.5 + 2.0 * splatted[288:320]

    def halo(source, turn, begin):
        for a, b in offsets:
            place = (a + 1) * 3 + b + 1

            @pl.when(inside(a, b))
            def _(a=a, b=b, place=place):
                if begin:
                    pltpu.make_async_remote_copy(
                        src_ref=source.at[pl.ds(8, 2)],
                        dst_ref=source.at[pl.ds(2 * (8 - place), 2)],
                        send_sem=halo_send.at[turn, place],
                        recv_sem=halo_recv.at[turn, 8 - place],
                        device_id=(wide + a, narrow + b),
                        device_id_type=MESH,
                    ).start()
                else:
                    got = source.at[pl.ds(2 * place, 2)]
                    pltpu.make_async_copy(got, got, halo_recv.at[turn, place]).wait()

    def near(brick, a, b, c):
        return near_ref[0, 0, brick, (a + 1) * 9 + (b + 1) * 3 + c + 1]

    cell_at = lax.broadcasted_iota(jnp.int32, (32, 256), 1)
    x_at = lax.broadcasted_iota(jnp.int32, (32, 256), 0) % 16
    y_at, z_at = cell_at // 16, cell_at % 16
    low_half = lax.broadcasted_iota(jnp.int32, (8, 128), 1) < 64

    def send_faces(turn, ends, packed):
        source = sources[turn]
        for brick in range(2):
            row = 16 * brick
            source[8 + brick, 0:8] = jnp.where(low_half, packed[row : row + 8], packed[row + 8 : row + 16])
            for k, x in enumerate((0, 15)):
                for half in range(2):
                    at = 8 + 2 * k + half
                    source[8 + brick, at : at + 1] = ends[row + x : row + x + 1, 128 * half : 128 * half + 128]
        halo(source, turn, True)

    def ends_of(source):
        rows = []
        for brick in range(2):
            low, high = near(brick, -1, 0, 0), near(brick, 1, 0, 0)
            low = jnp.concatenate([source[low, 10:11, :], source[low, 11:12, :]], 1)
            high = jnp.concatenate([source[high, 8:9, :], source[high, 9:10, :]], 1)
            rows.append((low, high))
        low = jnp.concatenate([jnp.broadcast_to(rows[brick][0], (16, 256)) for brick in range(2)], 0)
        high = jnp.concatenate([jnp.broadcast_to(rows[brick][1], (16, 256)) for brick in range(2)], 0)
        return low, high

    def merged(source, brick, a, rows, corners):
        lane = lax.broadcasted_iota(jnp.int32, (rows.stop - rows.start, 128), 1) % 64

        def beside(b, c):
            return source[near(brick, a, b, c), rows, :]

        faces = jnp.where(
            lane < 32,
            jnp.where(lane < 16, beside(1, 0), beside(-1, 0)),
            jnp.where(lane < 48, beside(0, 1), beside(0, -1)),
        )
        if not corners:
            return faces, faces
        corner = jnp.where(
            lane < 16,
            jnp.where(lane == 0, beside(1, 1), beside(1, -1)),
            jnp.where(lane == 16, beside(-1, 1), beside(-1, -1)),
        )
        return faces, corner

    def swap(values):
        return pltpu.roll(values, 64, 1)

    def faces_of(source, brick, corners):
        faces, corner = merged(source, brick, 0, slice(0, 8), corners)
        return jnp.concatenate(
            [jnp.where(low_half, faces, swap(corner)), jnp.where(low_half, swap(faces), corner)], 0
        )

    send_faces(
        0,
        vectors[0],
        jnp.where(
            lax.broadcasted_iota(jnp.int32, (32, 128), 1) % 64 < 32,
            exact_dot(vectors[1], pack_ref[...]),
            exact_dot(vectors[2], pack_ref[...]),
        ),
    )
    change = (
        jnp.where(x_at == 15, 0.0, pltpu.roll(vectors[0], 31, 0))
        - jnp.where(x_at == 0, 0.0, pltpu.roll(vectors[0], 1, 0))
        + jnp.where(y_at == 15, 0.0, pltpu.roll(vectors[1], 240, 1))
        - jnp.where(y_at == 0, 0.0, pltpu.roll(vectors[1], 16, 1))
        + jnp.where(z_at == 15, 0.0, pltpu.roll(vectors[2], 255, 1))
        - jnp.where(z_at == 0, 0.0, pltpu.roll(vectors[2], 1, 1))
    )
    halo(vector_src, 0, False)
    low, high = ends_of(vector_src)
    faces = jnp.concatenate([faces_of(vector_src, brick, False) for brick in range(2)], 0)
    change = (
        change
        + jnp.where(x_at == 15, high, 0.0)
        - jnp.where(x_at == 0, low, 0.0)
        + exact_dot(faces, slope_ref[...])
    )
    residual = -4.0 * change

    def pack(values):
        return exact_dot(values, pack_ref[...])

    def plane_sum(values):
        summed = values + 0.5 * (
            jnp.where(z_at == 0, 0.0, pltpu.roll(values, 1, 1))
            + jnp.where(z_at == 15, 0.0, pltpu.roll(values, 255, 1))
        )
        return summed + 0.5 * (
            jnp.where(y_at == 0, 0.0, pltpu.roll(summed, 16, 1))
            + jnp.where(y_at == 15, 0.0, pltpu.roll(summed, 240, 1))
        )

    def operator(turn, values):
        source = sources[1 + turn]
        inner = values + 0.5 * (
            jnp.where(x_at == 0, 0.0, pltpu.roll(values, 1, 0))
            + jnp.where(x_at == 15, 0.0, pltpu.roll(values, 31, 0))
        )
        own = shifted_diagonal * values - 2.0 * plane_sum(inner)
        halo(source, 1 + turn, False)
        low, high = ends_of(source)
        ends = plane_sum(jnp.where(x_at == 0, low, jnp.where(x_at == 15, high, 0.0)))
        row_at = lax.broadcasted_iota(jnp.int32, (16, 128), 0)
        half_row = lax.broadcasted_iota(jnp.int32, (1, 128), 1) < 64
        faces = []
        for brick in range(2):
            here = faces_of(source, brick, True)
            face, corner = merged(source, brick, -1, slice(7, 8), True)
            low = jnp.where(half_row, swap(face), corner)
            face, corner = merged(source, brick, 1, slice(0, 1), True)
            high = jnp.where(half_row, face, swap(corner))
            faces.append(
                here
                + 0.5
                * (
                    jnp.where(row_at == 0, low, pltpu.roll(here, 1, 0))
                    + jnp.where(row_at == 15, high, pltpu.roll(here, 15, 0))
                )
            )
        return own - ends - 2.0 * exact_dot(jnp.concatenate(faces, 0), weight_ref[...])

    def send_sums(turn, one, two):
        for row, values in enumerate((one, two)):
            summed = jnp.sum(values, axis=0, keepdims=True)
            part_out[turn, row : row + 1] = summed[:, :128] + summed[:, 128:]
        part_in[turn, pl.ds(me, 1)] = part_out[pl.ds(turn, 1)]

        each_device(
            lambda to: pltpu.make_async_remote_copy(
                src_ref=part_out.at[turn],
                dst_ref=part_in.at[turn, me],
                send_sem=part_send.at[turn],
                recv_sem=part_recv.at[turn],
                device_id=to,
                device_id_type=MESH,
            ).start()
        )

    def get_sums(turn):
        got = part_in.at[turn, pl.ds(0, devices - 1)]
        pltpu.make_async_copy(got, got, part_recv.at[turn]).wait()
        total = jnp.sum(jnp.sum(part_in[turn], axis=0), axis=1, keepdims=True)
        return total[0:1], total[1:2]

    send_faces(1, residual, pack(residual))
    image = operator(0, residual)

    packed = pack(image)
    send_faces(2, image, packed)
    send_sums(0, residual * residual, residual * image)
    second = operator(1, image)
    packed_second = pack(second)
    square_0, product = get_sums(0)
    step_0 = square_0 / product
    answer = step_0 * residual
    towards, towards_image, towards_second = residual, image, second
    residual = residual - step_0 * image
    image = image - step_0 * second
    packed = packed - step_0 * packed_second

    send_faces(3, image, packed)
    send_sums(1, residual * residual, residual * image)
    second = operator(2, image)
    square_1, product = get_sums(1)
    ratio = square_1 / square_0
    step_1 = square_1 / (product - ratio * square_1 / step_0)
    towards = residual + ratio * towards
    towards_image = image + ratio * towards_image
    towards_second = second + ratio * towards_second
    answer = answer + step_1 * towards
    residual = residual - step_1 * towards_image
    image = image - step_1 * towards_second

    send_sums(2, residual * residual, residual * image)
    square_2, product = get_sums(2)
    ratio = square_2 / square_1
    step_2 = square_2 / (product - ratio * square_2 / step_1)
    towards = residual + ratio * towards
    towards_image = image + ratio * towards_image
    answer = answer + step_2 * towards
    residual = residual - step_2 * towards_image

    for brick in range(2):
        for x in range(16):
            at = (0, 0, slice(brick, brick + 1), slice(256 * x, 256 * x + 256))
            solution_ref[at] = answer[16 * brick + x : 16 * brick + x + 1]
            residual_ref[at] = residual[16 * brick + x : 16 * brick + x + 1]

    sent = point_out.at[pl.ds(0, wides - 1)]
    pltpu.make_async_copy(sent, sent, point_send.at[0]).wait()
    for turn in range(3):
        sent = part_in.at[turn, pl.ds(0, devices - 1)]
        pltpu.make_async_copy(sent, sent, part_send.at[turn]).wait()
    for a, b in offsets:
        place = (a + 1) * 3 + b + 1

        @pl.when(inside(a, b))
        def _(place=place):
            for turn, source in enumerate(sources):
                sent = source.at[pl.ds(8, 2)]
                pltpu.make_async_copy(sent, sent, halo_send.at[turn, place]).wait()


def shards(wides, narrows, point_owner, point_cell, normals, strip_count, neighbours):
    points = point_cell.shape[0]
    devices = wides * narrows
    slots = 2 * points // wides
    vmem = pl.BlockSpec(memory_space=pltpu.VMEM)
    hbm = pl.BlockSpec(memory_space=pltpu.HBM)
    smem = pl.BlockSpec(memory_space=pltpu.SMEM)
    out = jax.ShapeDtypeStruct((1, 1, 2, 4096), F32)
    return pl.pallas_call(
        functools.partial(kernel, wides, narrows),
        out_shape=(out, out),
        in_specs=[hbm, hbm, hbm, smem, smem],
        out_specs=(vmem, vmem),
        scratch_shapes=[
            pltpu.VMEM((1, points), jnp.int32),
            pltpu.VMEM((1, points), jnp.int32),
            pltpu.VMEM((3, points), F32),
            pltpu.VMEM((256, 128), BF16),
            pltpu.VMEM((128, 256), BF16),
            pltpu.VMEM((128, 256), BF16),
            pltpu.VMEM((wides, 4, slots), F32),
            pltpu.VMEM((wides, 4, slots), F32),
            pltpu.VMEM((19, 12, 128), F32),
            pltpu.VMEM((19, 12, 128), F32),
            pltpu.VMEM((19, 12, 128), F32),
            pltpu.VMEM((19, 12, 128), F32),
            pltpu.VMEM((3, 2, 128), F32),
            pltpu.VMEM((3, devices, 2, 128), F32),
            pltpu.SemaphoreType.DMA((3,)),
            pltpu.SemaphoreType.DMA((1,)),
            pltpu.SemaphoreType.DMA((1,)),
            pltpu.SemaphoreType.DMA((4, 9)),
            pltpu.SemaphoreType.DMA((4, 9)),
            pltpu.SemaphoreType.DMA((3,)),
            pltpu.SemaphoreType.DMA((3,)),
        ],
        compiler_params=pltpu.CompilerParams(
            collective_id=0, has_side_effects=True, vmem_limit_bytes=32 * 1024 * 1024
        ),
    )(
        point_owner.reshape(1, points), point_cell.reshape(1, points), normals, strip_count, neighbours
    )


def solution(mesh):
    return jax.shard_map(
        functools.partial(shards, mesh.shape["wide"], mesh.shape["narrow"]),
        mesh=mesh,
        in_specs=(
            P(("wide", "narrow"), None),
            P(("wide", "narrow")),
            P(None, ("wide", "narrow")),
            P(("wide", "narrow")),
            P("wide", "narrow", None, None),
        ),
        out_specs=(P("wide", "narrow", None, None), P("wide", "narrow", None, None)),
        check_vma=False,
    )
```

```python
import functools

import jax
import jax.numpy as jnp
from jax import lax
from jax.experimental import pallas as pl
from jax.experimental.pallas import tpu as pltpu
from jax.sharding import PartitionSpec as P

MESH = pl.DeviceIdType.MESH
NT = (((1,), (1,)), ((), ()))
F32 = jnp.float32
BF16 = jnp.bfloat16


def split3(values):
    high = values.astype(BF16).astype(F32)
    rest = values - high
    middle = rest.astype(BF16).astype(F32)
    return high, middle, rest - middle


def one_if(condition):
    return jnp.where(condition, 1.0, 0.0)


def edge(offset):
    return one_if(offset == 0) + 0.5 * one_if((offset == 1) | (offset == -1))


def pack_matrix():
    cell = lax.broadcasted_iota(jnp.int32, (256, 128), 0)
    lane = lax.broadcasted_iota(jnp.int32, (256, 128), 1)
    side, k = (lane // 16) % 4, lane % 16
    wanted = jnp.where(side < 2, k + 240 * side, 16 * k + 15 * (side - 2))
    return one_if(cell == wanted).astype(BF16)


def halo_matrices():
    lane = lax.broadcasted_iota(jnp.int32, (128, 256), 0)
    cell = lax.broadcasted_iota(jnp.int32, (128, 256), 1)
    y, z = cell // 16, cell % 16
    side, k = lane // 16, lane % 16
    face_y = (one_if(side == 0) * one_if(y == 15), one_if(side == 1) * one_if(y == 0))
    face_z = (one_if(side == 2) * one_if(z == 15), one_if(side == 3) * one_if(z == 0))
    corner = (
        one_if((lane == 64) & (y == 15) & (z == 15))
        + one_if((lane == 79) & (y == 15) & (z == 0))
        + one_if((lane == 80) & (y == 0) & (z == 15))
        + one_if((lane == 95) & (y == 0) & (z == 0))
    )
    weight = 0.5 * ((face_y[0] + face_y[1]) * edge(z - k) + (face_z[0] + face_z[1]) * edge(y - k)) + 0.25 * corner
    slope = (face_y[0] - face_y[1]) * one_if(z == k) + (face_z[0] - face_z[1]) * one_if(y == k)
    return weight.astype(BF16), slope.astype(BF16)


def exact_dot(values, matrix):
    rows = values.shape[0]
    parts = jnp.concatenate(split3(values), 0).astype(BF16)
    summed = jnp.dot(parts, matrix, preferred_element_type=F32)
    return summed[:rows] + summed[rows : 2 * rows] + summed[2 * rows :]


def kernel(
    wides, narrows, owner_hbm, cell_hbm, normal_hbm, count_ref, near_ref, solution_ref, residual_ref,
    owner_ref, cell_ref, normal_ref, pack_ref, weight_ref, slope_ref,
    point_out, point_in, vector_src, field_0, field_1, field_2, part_out, part_in,
    in_sem, point_send, point_recv, halo_send, halo_recv, part_send, part_recv,
):
    devices = wides * narrows
    wide = lax.axis_index("wide")
    narrow = lax.axis_index("narrow")
    me = wide * narrows + narrow
    points = cell_ref.shape[1]
    slots = point_out.shape[2]
    loads = [
        pltpu.make_async_copy(source, target, in_sem.at[k])
        for k, (source, target) in enumerate(
            ((owner_hbm, owner_ref), (cell_hbm, cell_ref), (normal_hbm, normal_ref))
        )
    ]
    for load in loads:
        load.start()
    barrier = pltpu.get_barrier_semaphore()

    def after(at, step, count):
        return jnp.where(at + step >= count, at + step - count, at + step)

    def each_device(act):
        if devices > 64:

            @pl.loop(1, devices)
            def _(k):
                other = lax.rem(me + k, devices)
                act((other // narrows, lax.rem(other, narrows)))

            return
        for to_wide in far_first + [wide]:
            for to_narrow in narrow_after[::-1]:
                if to_wide is not wide or to_narrow is not narrow:
                    act((to_wide, to_narrow))

    far_first = []
    if wides & (wides - 1):
        far_first = [after(wide, k, wides) for k in range(1, wides)]
    else:
        flips = []
        bit = 1
        while bit < wides:
            flips.append((1 - 2 * (lax.div(wide, bit) % 2)) * bit)
            bit = 2 * bit
        for k in range(wides - 1, 0, -1):
            far_first.append(wide + sum(flip for j, flip in enumerate(flips) if k >> j & 1))
    narrow_after = [narrow] + [after(narrow, k, narrows) for k in range(1, narrows)]
    each_device(lambda to: pl.semaphore_signal(barrier, inc=1, device_id=to, device_id_type=MESH))

    offsets = [(a, b) for a in (1, -1, 0) for b in (-1, 1, 0) if (a, b) != (0, 0)]

    def inside(a, b):
        return (wide + a >= 0) & (wide + a < wides) & (narrow + b >= 0) & (narrow + b < narrows)

    sources = (vector_src, field_0, field_1, field_2)
    for source in sources:
        source[18] = jnp.zeros((12, 128), F32)
    for a, b in offsets:
        place = (a + 1) * 3 + b + 1

        @pl.when(jnp.logical_not(inside(a, b)))
        def _(place=place):
            for source in sources:
                source[2 * place : 2 * place + 2] = jnp.zeros((2, 12, 128), F32)

    for load in loads:
        load.wait()

    owner = owner_ref[...]
    live = lax.broadcasted_iota(jnp.int32, (1, points), 1) < count_ref[0]
    owned = lax.broadcasted_iota(jnp.int32, (wides, points), 0) == owner
    owner_hot = one_if(owned)
    blocks = points // 128
    stacked = jnp.concatenate([owner_hot[:, k * 128 : (k + 1) * 128] for k in range(blocks)], 0)
    earlier = jnp.where(
        lax.broadcasted_iota(jnp.int32, (128, 256), 0) < lax.broadcasted_iota(jnp.int32, (128, 256), 1),
        1.0,
        0.0,
    )
    counted = jnp.dot(stacked.astype(BF16), earlier.astype(BF16), preferred_element_type=F32)
    ranks = []
    before = jnp.zeros((wides, 128), F32)
    for k in range(blocks):
        rows = slice(k * wides, (k + 1) * wides)
        ranks.append(
            jnp.sum(stacked[rows] * (counted[rows, :128] + before), axis=0, keepdims=True)
        )
        before = before + counted[rows, 128:]
    rank = jnp.concatenate(ranks, 1).astype(jnp.int32)
    code = jnp.where(live, cell_ref[...] + 1, 0)
    rows = [lax.shift_right_logical(code, 8).astype(F32), (code & 255).astype(F32)]
    for c in range(3):
        rows.extend(split3(normal_ref[c : c + 1]))
    weighted = jnp.concatenate([jnp.where(owned, row, 0.0) for row in rows], 0).astype(BF16)
    rank_hot = one_if(lax.broadcasted_iota(jnp.int32, (slots, points), 0) == rank).astype(BF16)
    moved = lax.dot_general(weighted, rank_hot, NT, preferred_element_type=F32)
    moved = [moved[k * wides : (k + 1) * wides] for k in range(11)]
    values = [moved[2 + 3 * c] + moved[3 + 3 * c] + moved[4 + 3 * c] for c in range(3)]
    values.append(256.0 * moved[0] + moved[1])
    for k in range(wides):
        for c in range(4):
            point_out[k, c : c + 1] = values[c][k : k + 1]

    pl.semaphore_wait(barrier, devices - 1)

    for other in far_first:
        pltpu.make_async_remote_copy(
            src_ref=point_out.at[other],
            dst_ref=point_in.at[wide],
            send_sem=point_send.at[0],
            recv_sem=point_recv.at[0],
            device_id=(other, narrow),
            device_id_type=MESH,
        ).start()

    pack_ref[...] = pack_matrix()
    weight_ref[...], slope_ref[...] = halo_matrices()
    point_in[pl.ds(wide, 1)] = point_out[pl.ds(wide, 1)]
    arrived = point_in.at[pl.ds(0, wides - 1)]
    pltpu.make_async_copy(arrived, arrived, point_recv.at[0]).wait()

    group = 8 if slots % 128 == 0 and wides % 8 == 0 else 1
    splatted = jnp.zeros((320, 256), F32)
    for k in range(0, wides, group):
        got = jnp.concatenate([point_in[k + j] for j in range(group)], 1)
        width = group * slots
        cell = got[3:4].astype(jnp.int32) - 1
        row_hot = lax.broadcasted_iota(jnp.int32, (32, width), 0) == lax.shift_right_arithmetic(cell, 8)
        lane_hot = lax.broadcasted_iota(jnp.int32, (256, width), 0) == (cell & 255)
        weights = []
        for c in range(3):
            weights.extend(split3(got[c : c + 1]))
        weights.append(jnp.ones((1, width), F32))
        weighted = jnp.concatenate([jnp.where(row_hot, w, 0.0) for w in weights], 0).astype(BF16)
        splatted = splatted + lax.dot_general(
            weighted, jnp.where(lane_hot, 1.0, 0.0).astype(BF16), NT, preferred_element_type=F32
        )
    vectors = [
        splatted[96 * c : 96 * c + 32] + splatted[96 * c + 32 : 96 * c + 64] + splatted[96 * c + 64 : 96 * c + 96]
        for c in range(3)
    ]
    shifted_diagonal = 16.5 + 2.0 * splatted[288:320]

    def halo(source, turn, begin):
        for a, b in offsets:
            place = (a + 1) * 3 + b + 1

            @pl.when(inside(a, b))
            def _(a=a, b=b, place=place):
                if begin:
                    pltpu.make_async_remote_copy(
                        src_ref=source.at[pl.ds(8, 2)],
                        dst_ref=source.at[pl.ds(2 * (8 - place), 2)],
                        send_sem=halo_send.at[turn, place],
                        recv_sem=halo_recv.at[turn, 8 - place],
                        device_id=(wide + a, narrow + b),
                        device_id_type=MESH,
                    ).start()
                else:
                    got = source.at[pl.ds(2 * place, 2)]
                    pltpu.make_async_copy(got, got, halo_recv.at[turn, place]).wait()

    def near(brick, a, b, c):
        return near_ref[0, 0, brick, (a + 1) * 9 + (b + 1) * 3 + c + 1]

    cell_at = lax.broadcasted_iota(jnp.int32, (32, 256), 1)
    x_at = lax.broadcasted_iota(jnp.int32, (32, 256), 0) % 16
    y_at, z_at = cell_at // 16, cell_at % 16
    low_half = lax.broadcasted_iota(jnp.int32, (8, 128), 1) < 64

    def send_faces(turn, ends, packed):
        source = sources[turn]
        for brick in range(2):
            row = 16 * brick
            source[8 + brick, 0:8] = jnp.where(low_half, packed[row : row + 8], packed[row + 8 : row + 16])
            for k, x in enumerate((0, 15)):
                for half in range(2):
                    at = 8 + 2 * k + half
                    source[8 + brick, at : at + 1] = ends[row + x : row + x + 1, 128 * half : 128 * half + 128]
        halo(source, turn, True)

    def ends_of(source):
        rows = []
        for brick in range(2):
            low, high = near(brick, -1, 0, 0), near(brick, 1, 0, 0)
            low = jnp.concatenate([source[low, 10:11, :], source[low, 11:12, :]], 1)
            high = jnp.concatenate([source[high, 8:9, :], source[high, 9:10, :]], 1)
            rows.append((low, high))
        low = jnp.concatenate([jnp.broadcast_to(rows[brick][0], (16, 256)) for brick in range(2)], 0)
        high = jnp.concatenate([jnp.broadcast_to(rows[brick][1], (16, 256)) for brick in range(2)], 0)
        return low, high

    def merged(source, brick, a, rows, corners):
        lane = lax.broadcasted_iota(jnp.int32, (rows.stop - rows.start, 128), 1) % 64

        def beside(b, c):
            return source[near(brick, a, b, c), rows, :]

        faces = jnp.where(
            lane < 32,
            jnp.where(lane < 16, beside(1, 0), beside(-1, 0)),
            jnp.where(lane < 48, beside(0, 1), beside(0, -1)),
        )
        if not corners:
            return faces, faces
        corner = jnp.where(
            lane < 16,
            jnp.where(lane == 0, beside(1, 1), beside(1, -1)),
            jnp.where(lane == 16, beside(-1, 1), beside(-1, -1)),
        )
        return faces, corner

    def swap(values):
        return pltpu.roll(values, 64, 1)

    def faces_of(source, brick, corners):
        faces, corner = merged(source, brick, 0, slice(0, 8), corners)
        return jnp.concatenate(
            [jnp.where(low_half, faces, swap(corner)), jnp.where(low_half, swap(faces), corner)], 0
        )

    send_faces(
        0,
        vectors[0],
        jnp.where(
            lax.broadcasted_iota(jnp.int32, (32, 128), 1) % 64 < 32,
            exact_dot(vectors[1], pack_ref[...]),
            exact_dot(vectors[2], pack_ref[...]),
        ),
    )
    change = (
        jnp.where(x_at == 15, 0.0, pltpu.roll(vectors[0], 31, 0))
        - jnp.where(x_at == 0, 0.0, pltpu.roll(vectors[0], 1, 0))
        + jnp.where(y_at == 15, 0.0, pltpu.roll(vectors[1], 240, 1))
        - jnp.where(y_at == 0, 0.0, pltpu.roll(vectors[1], 16, 1))
        + jnp.where(z_at == 15, 0.0, pltpu.roll(vectors[2], 255, 1))
        - jnp.where(z_at == 0, 0.0, pltpu.roll(vectors[2], 1, 1))
    )
    halo(vector_src, 0, False)
    low, high = ends_of(vector_src)
    faces = jnp.concatenate([faces_of(vector_src, brick, False) for brick in range(2)], 0)
    change = (
        change
        + jnp.where(x_at == 15, high, 0.0)
        - jnp.where(x_at == 0, low, 0.0)
        + exact_dot(faces, slope_ref[...])
    )
    residual = -4.0 * change

    def pack(values):
        return exact_dot(values, pack_ref[...])

    def plane_sum(values):
        summed = values + 0.5 * (
            jnp.where(z_at == 0, 0.0, pltpu.roll(values, 1, 1))
            + jnp.where(z_at == 15, 0.0, pltpu.roll(values, 255, 1))
        )
        return summed + 0.5 * (
            jnp.where(y_at == 0, 0.0, pltpu.roll(summed, 16, 1))
            + jnp.where(y_at == 15, 0.0, pltpu.roll(summed, 240, 1))
        )

    def operator(turn, values):
        source = sources[1 + turn]
        inner = values + 0.5 * (
            jnp.where(x_at == 0, 0.0, pltpu.roll(values, 1, 0))
            + jnp.where(x_at == 15, 0.0, pltpu.roll(values, 31, 0))
        )
        own = shifted_diagonal * values - 2.0 * plane_sum(inner)
        halo(source, 1 + turn, False)
        low, high = ends_of(source)
        ends = plane_sum(jnp.where(x_at == 0, low, jnp.where(x_at == 15, high, 0.0)))
        row_at = lax.broadcasted_iota(jnp.int32, (16, 128), 0)
        half_row = lax.broadcasted_iota(jnp.int32, (1, 128), 1) < 64
        faces = []
        for brick in range(2):
            here = faces_of(source, brick, True)
            face, corner = merged(source, brick, -1, slice(7, 8), True)
            low = jnp.where(half_row, swap(face), corner)
            face, corner = merged(source, brick, 1, slice(0, 1), True)
            high = jnp.where(half_row, face, swap(corner))
            faces.append(
                here
                + 0.5
                * (
                    jnp.where(row_at == 0, low, pltpu.roll(here, 1, 0))
                    + jnp.where(row_at == 15, high, pltpu.roll(here, 15, 0))
                )
            )
        return own - ends - 2.0 * exact_dot(jnp.concatenate(faces, 0), weight_ref[...])

    def send_sums(turn, products):
        for row, values in enumerate(products):
            summed = jnp.sum(values, axis=0, keepdims=True)
            part_out[turn, row : row + 1] = summed[:, :128] + summed[:, 128:]
        part_in[turn, pl.ds(me, 1)] = part_out[pl.ds(turn, 1)]
        each_device(
            lambda to: pltpu.make_async_remote_copy(
                src_ref=part_out.at[turn],
                dst_ref=part_in.at[turn, me],
                send_sem=part_send.at[turn],
                recv_sem=part_recv.at[turn],
                device_id=to,
                device_id_type=MESH,
            ).start()
        )

    def get_sums(turn):
        got = part_in.at[turn, pl.ds(0, devices - 1)]
        pltpu.make_async_copy(got, got, part_recv.at[turn]).wait()
        total = jnp.sum(jnp.sum(part_in[turn], axis=0), axis=1, keepdims=True)
        return total[0:1], total[1:2], total[2:3], total[3:4]

    send_faces(1, residual, pack(residual))
    image = operator(0, residual)

    send_faces(2, image, pack(image))
    second = operator(1, image)

    send_faces(3, second, pack(second))
    send_sums(0, (residual * residual, residual * image, image * image, image * second))
    third = operator(2, second)
    square_0, product, square_image, product_image = get_sums(0)
    step_0 = square_0 / product
    square_1 = step_0 * step_0 * square_image - square_0
    product = product - 2.0 * step_0 * square_image + step_0 * step_0 * product_image
    ratio = square_1 / square_0
    step_1 = square_1 / (product - ratio * square_1 / step_0)
    answer = step_0 * residual
    towards, towards_image, towards_second = residual, image, second
    residual = residual - step_0 * image
    image = image - step_0 * second
    second = second - step_0 * third
    towards = residual + ratio * towards
    towards_image = image + ratio * towards_image
    towards_second = second + ratio * towards_second
    answer = answer + step_1 * towards
    residual = residual - step_1 * towards_image
    image = image - step_1 * towards_second

    square, product = residual * residual, residual * image
    send_sums(1, (square, product, square, product))
    square_2, product, _, _ = get_sums(1)
    ratio = square_2 / square_1
    step_2 = square_2 / (product - ratio * square_2 / step_1)
    towards = residual + ratio * towards
    towards_image = image + ratio * towards_image
    answer = answer + step_2 * towards
    residual = residual - step_2 * towards_image

    for brick in range(2):
        for x in range(16):
            at = (0, 0, slice(brick, brick + 1), slice(256 * x, 256 * x + 256))
            solution_ref[at] = answer[16 * brick + x : 16 * brick + x + 1]
            residual_ref[at] = residual[16 * brick + x : 16 * brick + x + 1]

    sent = point_out.at[pl.ds(0, wides - 1)]
    pltpu.make_async_copy(sent, sent, point_send.at[0]).wait()
    for turn in range(2):
        sent = part_in.at[turn, pl.ds(0, devices - 1)]
        pltpu.make_async_copy(sent, sent, part_send.at[turn]).wait()
    for a, b in offsets:
        place = (a + 1) * 3 + b + 1

        @pl.when(inside(a, b))
        def _(place=place):
            for turn, source in enumerate(sources):
                sent = source.at[pl.ds(8, 2)]
                pltpu.make_async_copy(sent, sent, halo_send.at[turn, place]).wait()


def shards(wides, narrows, point_owner, point_cell, normals, strip_count, neighbours):
    points = point_cell.shape[0]
    devices = wides * narrows
    slots = 2 * points // wides
    vmem = pl.BlockSpec(memory_space=pltpu.VMEM)
    hbm = pl.BlockSpec(memory_space=pltpu.HBM)
    smem = pl.BlockSpec(memory_space=pltpu.SMEM)
    out = jax.ShapeDtypeStruct((1, 1, 2, 4096), F32)
    return pl.pallas_call(
        functools.partial(kernel, wides, narrows),
        out_shape=(out, out),
        in_specs=[hbm, hbm, hbm, smem, smem],
        out_specs=(vmem, vmem),
        scratch_shapes=[
            pltpu.VMEM((1, points), jnp.int32),
            pltpu.VMEM((1, points), jnp.int32),
            pltpu.VMEM((3, points), F32),
            pltpu.VMEM((256, 128), BF16),
            pltpu.VMEM((128, 256), BF16),
            pltpu.VMEM((128, 256), BF16),
            pltpu.VMEM((wides, 4, slots), F32),
            pltpu.VMEM((wides, 4, slots), F32),
            pltpu.VMEM((19, 12, 128), F32),
            pltpu.VMEM((19, 12, 128), F32),
            pltpu.VMEM((19, 12, 128), F32),
            pltpu.VMEM((19, 12, 128), F32),
            pltpu.VMEM((2, 4, 128), F32),
            pltpu.VMEM((2, devices, 4, 128), F32),
            pltpu.SemaphoreType.DMA((3,)),
            pltpu.SemaphoreType.DMA((1,)),
            pltpu.SemaphoreType.DMA((1,)),
            pltpu.SemaphoreType.DMA((4, 9)),
            pltpu.SemaphoreType.DMA((4, 9)),
            pltpu.SemaphoreType.DMA((3,)),
            pltpu.SemaphoreType.DMA((3,)),
        ],
        compiler_params=pltpu.CompilerParams(
            collective_id=0, has_side_effects=True, vmem_limit_bytes=32 * 1024 * 1024
        ),
    )(
        point_owner.reshape(1, points), point_cell.reshape(1, points), normals, strip_count, neighbours
    )


def solution(mesh):
    return jax.shard_map(
        functools.partial(shards, mesh.shape["wide"], mesh.shape["narrow"]),
        mesh=mesh,
        in_specs=(
            P(("wide", "narrow"), None),
            P(("wide", "narrow")),
            P(None, ("wide", "narrow")),
            P(("wide", "narrow")),
            P("wide", "narrow", None, None),
        ),
        out_specs=(P("wide", "narrow", None, None), P("wide", "narrow", None, None)),
        check_vma=False,
    )
```

```python
import functools

import jax
import jax.numpy as jnp
from jax import lax
from jax.experimental import pallas as pl
from jax.experimental.pallas import tpu as pltpu
from jax.sharding import PartitionSpec as P

MESH = pl.DeviceIdType.MESH
NT = (((1,), (1,)), ((), ()))
F32 = jnp.float32
BF16 = jnp.bfloat16


def split3(values):
    high = values.astype(BF16).astype(F32)
    rest = values - high
    middle = rest.astype(BF16).astype(F32)
    return high, middle, rest - middle


def one_if(condition):
    return jnp.where(condition, 1.0, 0.0)


def edge(offset):
    return one_if(offset == 0) + 0.5 * one_if((offset == 1) | (offset == -1))


def pack_matrix():
    cell = lax.broadcasted_iota(jnp.int32, (256, 128), 0)
    lane = lax.broadcasted_iota(jnp.int32, (256, 128), 1)
    side, k = (lane // 16) % 4, lane % 16
    wanted = jnp.where(side < 2, k + 240 * side, 16 * k + 15 * (side - 2))
    return one_if(cell == wanted).astype(BF16)


def halo_matrices():
    lane = lax.broadcasted_iota(jnp.int32, (128, 256), 0)
    cell = lax.broadcasted_iota(jnp.int32, (128, 256), 1)
    y, z = cell // 16, cell % 16
    side, k = lane // 16, lane % 16
    face_y = (one_if(side == 0) * one_if(y == 15), one_if(side == 1) * one_if(y == 0))
    face_z = (one_if(side == 2) * one_if(z == 15), one_if(side == 3) * one_if(z == 0))
    corner = (
        one_if((lane == 64) & (y == 15) & (z == 15))
        + one_if((lane == 79) & (y == 15) & (z == 0))
        + one_if((lane == 80) & (y == 0) & (z == 15))
        + one_if((lane == 95) & (y == 0) & (z == 0))
    )
    weight = 0.5 * ((face_y[0] + face_y[1]) * edge(z - k) + (face_z[0] + face_z[1]) * edge(y - k)) + 0.25 * corner
    slope = (face_y[0] - face_y[1]) * one_if(z == k) + (face_z[0] - face_z[1]) * one_if(y == k)
    return weight.astype(BF16), slope.astype(BF16)


def plane_matrix():
    one = lax.broadcasted_iota(jnp.int32, (256, 256), 0)
    two = lax.broadcasted_iota(jnp.int32, (256, 256), 1)
    return (edge(one // 16 - two // 16) * edge(one % 16 - two % 16)).astype(BF16)


def with_packed(matrix, selection):
    return jnp.concatenate([matrix, jnp.dot(matrix, selection, preferred_element_type=F32).astype(BF16)], 1)


def exact_dot(values, matrix):
    rows = values.shape[0]
    parts = jnp.concatenate(split3(values), 0).astype(BF16)
    summed = jnp.dot(parts, matrix, preferred_element_type=F32)
    return summed[:rows] + summed[rows : 2 * rows] + summed[2 * rows :]


def kernel(
    wides, narrows, owner_hbm, cell_hbm, normal_hbm, count_ref, near_ref, solution_ref, residual_ref,
    owner_ref, cell_ref, normal_ref, pack_ref, weight_ref, slope_ref, plane_ref,
    point_out, point_in, vector_src, field_0, field_1, field_2, part_out, part_in,
    in_sem, point_send, point_recv, halo_send, halo_recv, part_send, part_recv,
):
    devices = wides * narrows
    wide = lax.axis_index("wide")
    narrow = lax.axis_index("narrow")
    me = wide * narrows + narrow
    points = cell_ref.shape[1]
    slots = point_out.shape[2]
    loads = [
        pltpu.make_async_copy(source, target, in_sem.at[k])
        for k, (source, target) in enumerate(
            ((owner_hbm, owner_ref), (cell_hbm, cell_ref), (normal_hbm, normal_ref))
        )
    ]
    for load in loads:
        load.start()
    sources = (vector_src, field_0, field_1, field_2)
    for source in sources:
        for place in range(19):
            if place // 2 != 4:
                source[place] = jnp.zeros((12, 128), F32)

    barrier = pltpu.get_barrier_semaphore()

    def after(at, step, count):
        return jnp.where(at + step >= count, at + step - count, at + step)

    def each_device(act):
        if devices > 64:

            @pl.loop(1, devices)
            def _(k):
                other = lax.rem(me + k, devices)
                act((other // narrows, lax.rem(other, narrows)))

            return
        for to_wide in far_first + [wide]:
            for to_narrow in narrow_after[::-1]:
                if to_wide is not wide or to_narrow is not narrow:
                    act((to_wide, to_narrow))

    far_first = []
    if wides & (wides - 1):
        far_first = [after(wide, k, wides) for k in range(1, wides)]
    else:
        flips = []
        bit = 1
        while bit < wides:
            flips.append((1 - 2 * (lax.div(wide, bit) % 2)) * bit)
            bit = 2 * bit
        for k in range(wides - 1, 0, -1):
            far_first.append(wide + sum(flip for j, flip in enumerate(flips) if k >> j & 1))
    narrow_after = [narrow] + [after(narrow, k, narrows) for k in range(1, narrows)]
    each_device(lambda to: pl.semaphore_signal(barrier, inc=1, device_id=to, device_id_type=MESH))

    if narrows == 2:
        turns = (1 - 2 * narrow,)
    else:
        turns = (-1, 1)
    groups = []
    for a in (1, -1):
        there = (wide + a >= 0) & (wide + a < wides)
        if narrows == 2:
            groups.append((there, [(a, turns[0]), (a, 0)]))
        else:
            groups.append((there, [(a, 0)]))
            for b in turns:
                groups.append((there & (narrow + b >= 0) & (narrow + b < narrows), [(a, b)]))
    for b in turns:
        groups.append((None if narrows == 2 else (narrow + b >= 0) & (narrow + b < narrows), [(0, b)]))

    def each_beside(act):
        for there, peers in groups:

            def body(peers=peers):
                for a, b in peers:
                    act(a, b, (a + 1) * 3 + b + 1)

            if there is None:
                body()
            else:
                pl.when(there)(body)

    for load in loads:
        load.wait()

    owner = owner_ref[...]
    live = lax.broadcasted_iota(jnp.int32, (1, points), 1) < count_ref[0]
    owned = lax.broadcasted_iota(jnp.int32, (wides, points), 0) == owner
    owner_hot = one_if(owned)
    blocks = points // 128
    stacked = jnp.concatenate([owner_hot[:, k * 128 : (k + 1) * 128] for k in range(blocks)], 0)
    earlier = jnp.where(
        lax.broadcasted_iota(jnp.int32, (128, 256), 0) < lax.broadcasted_iota(jnp.int32, (128, 256), 1),
        1.0,
        0.0,
    )
    counted = jnp.dot(stacked.astype(BF16), earlier.astype(BF16), preferred_element_type=F32)
    ranks = []
    before = jnp.zeros((wides, 128), F32)
    for k in range(blocks):
        rows = slice(k * wides, (k + 1) * wides)
        ranks.append(
            jnp.sum(stacked[rows] * (counted[rows, :128] + before), axis=0, keepdims=True)
        )
        before = before + counted[rows, 128:]
    rank = jnp.concatenate(ranks, 1).astype(jnp.int32)
    code = jnp.where(live, cell_ref[...] + 1, 0)
    rows = [lax.shift_right_logical(code, 8).astype(F32), (code & 255).astype(F32)]
    for c in range(3):
        rows.extend(split3(normal_ref[c : c + 1]))
    weighted = jnp.concatenate([jnp.where(owned, row, 0.0) for row in rows], 0).astype(BF16)
    rank_hot = one_if(lax.broadcasted_iota(jnp.int32, (slots, points), 0) == rank).astype(BF16)
    moved = lax.dot_general(weighted, rank_hot, NT, preferred_element_type=F32)
    moved = [moved[k * wides : (k + 1) * wides] for k in range(11)]
    values = [moved[2 + 3 * c] + moved[3 + 3 * c] + moved[4 + 3 * c] for c in range(3)]
    values.append(256.0 * moved[0] + moved[1])
    for k in range(wides):
        for c in range(4):
            point_out[k, c : c + 1] = values[c][k : k + 1]

    pl.semaphore_wait(barrier, devices - 1)

    for other in far_first:
        pltpu.make_async_remote_copy(
            src_ref=point_out.at[other],
            dst_ref=point_in.at[wide],
            send_sem=point_send.at[0],
            recv_sem=point_recv.at[0],
            device_id=(other, narrow),
            device_id_type=MESH,
        ).start()

    pack_ref[...] = pack_matrix()
    weight, slope = halo_matrices()
    weight_ref[...] = with_packed(weight, pack_ref[...])
    slope_ref[...] = with_packed(slope, pack_ref[...])
    plane_ref[...] = with_packed(plane_matrix(), pack_ref[...])
    point_in[pl.ds(wide, 1)] = point_out[pl.ds(wide, 1)]
    arrived = point_in.at[pl.ds(0, wides - 1)]
    pltpu.make_async_copy(arrived, arrived, point_recv.at[0]).wait()

    group = 8 if slots % 128 == 0 and wides % 8 == 0 else 1
    splatted = jnp.zeros((320, 256), F32)
    for k in range(0, wides, group):
        got = jnp.concatenate([point_in[k + j] for j in range(group)], 1)
        width = group * slots
        cell = got[3:4].astype(jnp.int32) - 1
        row_hot = lax.broadcasted_iota(jnp.int32, (32, width), 0) == lax.shift_right_arithmetic(cell, 8)
        lane_hot = lax.broadcasted_iota(jnp.int32, (256, width), 0) == (cell & 255)
        weights = []
        for c in range(3):
            weights.extend(split3(got[c : c + 1]))
        weights.append(jnp.ones((1, width), F32))
        weighted = jnp.concatenate([jnp.where(row_hot, w, 0.0) for w in weights], 0).astype(BF16)
        splatted = splatted + lax.dot_general(
            weighted, jnp.where(lane_hot, 1.0, 0.0).astype(BF16), NT, preferred_element_type=F32
        )
    vectors = [
        splatted[96 * c : 96 * c + 32] + splatted[96 * c + 32 : 96 * c + 64] + splatted[96 * c + 64 : 96 * c + 96]
        for c in range(3)
    ]
    shifted_diagonal = 16.5 + 2.0 * splatted[288:320]

    def halo_start(source, turn):
        def start(a, b, place):
            pltpu.make_async_remote_copy(
                src_ref=source.at[pl.ds(8, 2)],
                dst_ref=source.at[pl.ds(2 * (8 - place), 2)],
                send_sem=halo_send.at[turn, place],
                recv_sem=halo_recv.at[turn, 8 - place],
                device_id=(wide + a, narrow + b),
                device_id_type=MESH,
            ).start()

        each_beside(start)

    def halo_wait(source, turn):
        def wait(a, b, place):
            got = source.at[pl.ds(2 * place, 2)]
            pltpu.make_async_copy(got, got, halo_recv.at[turn, place]).wait()

        each_beside(wait)

    def near(brick, a, b, c):
        return near_ref[0, 0, brick, (a + 1) * 9 + (b + 1) * 3 + c + 1]

    cell_at = lax.broadcasted_iota(jnp.int32, (32, 256), 1)
    x_at = lax.broadcasted_iota(jnp.int32, (32, 256), 0) % 16
    y_at, z_at = cell_at // 16, cell_at % 16
    low_half = lax.broadcasted_iota(jnp.int32, (8, 128), 1) < 64

    def send_faces(turn, ends, packed):
        source = sources[turn]
        for brick in range(2):
            row = 16 * brick
            source[8 + brick, 0:8] = jnp.where(low_half, packed[row : row + 8], packed[row + 8 : row + 16])
            for k, x in enumerate((0, 15)):
                for half in range(2):
                    at = 8 + 2 * k + half
                    source[8 + brick, at : at + 1] = ends[row + x : row + x + 1, 128 * half : 128 * half + 128]
        halo_start(source, turn)

    def ends_of(source):
        rows = []
        for brick in range(2):
            low, high = near(brick, -1, 0, 0), near(brick, 1, 0, 0)
            rows.append(jnp.concatenate([source[low, 10:11, :], source[low, 11:12, :]], 1))
            rows.append(jnp.concatenate([source[high, 8:9, :], source[high, 9:10, :]], 1))
        return jnp.concatenate(rows + [jnp.zeros((4, 256), F32)], 0)

    x_wide = lax.broadcasted_iota(jnp.int32, (16, 384), 0)

    def at_ends(rows, sign):
        return jnp.concatenate(
            [
                jnp.where(
                    x_wide == 0, sign * rows[2 * k : 2 * k + 1], jnp.where(x_wide == 15, rows[2 * k + 1 : 2 * k + 2], 0.0)
                )
                for k in range(2)
            ],
            0,
        )

    def pack(values):
        return exact_dot(values, pack_ref[...])

    def merged(source, brick, a, rows, corners):
        lane = lax.broadcasted_iota(jnp.int32, (rows.stop - rows.start, 128), 1) % 64

        def beside(b, c):
            return source[near(brick, a, b, c), rows, :]

        faces = jnp.where(
            lane < 32,
            jnp.where(lane < 16, beside(1, 0), beside(-1, 0)),
            jnp.where(lane < 48, beside(0, 1), beside(0, -1)),
        )
        if not corners:
            return faces, faces
        corner = jnp.where(
            lane < 16,
            jnp.where(lane == 0, beside(1, 1), beside(1, -1)),
            jnp.where(lane == 16, beside(-1, 1), beside(-1, -1)),
        )
        return faces, corner

    def swap(values):
        return pltpu.roll(values, 64, 1)

    def faces_of(source, brick, corners):
        faces, corner = merged(source, brick, 0, slice(0, 8), corners)
        return jnp.concatenate(
            [jnp.where(low_half, faces, swap(corner)), jnp.where(low_half, swap(faces), corner)], 0
        )

    send_faces(
        0,
        vectors[0],
        jnp.where(
            lax.broadcasted_iota(jnp.int32, (32, 128), 1) % 64 < 32,
            exact_dot(vectors[1], pack_ref[...]),
            exact_dot(vectors[2], pack_ref[...]),
        ),
    )
    change = (
        jnp.where(x_at == 15, 0.0, pltpu.roll(vectors[0], 31, 0))
        - jnp.where(x_at == 0, 0.0, pltpu.roll(vectors[0], 1, 0))
        + jnp.where(y_at == 15, 0.0, pltpu.roll(vectors[1], 240, 1))
        - jnp.where(y_at == 0, 0.0, pltpu.roll(vectors[1], 16, 1))
        + jnp.where(z_at == 15, 0.0, pltpu.roll(vectors[2], 255, 1))
        - jnp.where(z_at == 0, 0.0, pltpu.roll(vectors[2], 1, 1))
    )
    change = jnp.concatenate([change, pack(change)], 1)
    halo_wait(vector_src, 0)
    ends = ends_of(vector_src)
    faces = jnp.concatenate([faces_of(vector_src, brick, False) for brick in range(2)], 0)
    change = (
        change
        + at_ends(jnp.concatenate([ends, pack(ends)], 1), -1.0)
        + exact_dot(faces, slope_ref[...])
    )
    change = -4.0 * change
    residual, packed = change[:, :256], change[:, 256:]

    def plane_sum(values):
        summed = values + 0.5 * (
            jnp.where(z_at == 0, 0.0, pltpu.roll(values, 1, 1))
            + jnp.where(z_at == 15, 0.0, pltpu.roll(values, 255, 1))
        )
        return summed + 0.5 * (
            jnp.where(y_at == 0, 0.0, pltpu.roll(summed, 16, 1))
            + jnp.where(y_at == 15, 0.0, pltpu.roll(summed, 240, 1))
        )

    def operator(turn, values):
        source = sources[1 + turn]
        inner = values + 0.5 * (
            jnp.where(x_at == 0, 0.0, pltpu.roll(values, 1, 0))
            + jnp.where(x_at == 15, 0.0, pltpu.roll(values, 31, 0))
        )
        own = shifted_diagonal * values - 2.0 * plane_sum(inner)
        own = jnp.concatenate([own, pack(own)], 1)
        halo_wait(source, 1 + turn)
        ends = at_ends(exact_dot(ends_of(source), plane_ref[...]), 1.0)
        row_at = lax.broadcasted_iota(jnp.int32, (16, 128), 0)
        half_row = lax.broadcasted_iota(jnp.int32, (1, 128), 1) < 64
        faces = []
        for brick in range(2):
            here = faces_of(source, brick, True)
            face, corner = merged(source, brick, -1, slice(7, 8), True)
            low = jnp.where(half_row, swap(face), corner)
            face, corner = merged(source, brick, 1, slice(0, 1), True)
            high = jnp.where(half_row, face, swap(corner))
            faces.append(
                here
                + 0.5
                * (
                    jnp.where(row_at == 0, low, pltpu.roll(here, 1, 0))
                    + jnp.where(row_at == 15, high, pltpu.roll(here, 15, 0))
                )
            )
        both = own - ends - 2.0 * exact_dot(jnp.concatenate(faces, 0), weight_ref[...])
        return both[:, :256], both[:, 256:]

    def send_sums(turn, one, two):
        for row, values in enumerate((one, two)):
            summed = jnp.sum(values, axis=0, keepdims=True)
            part_out[turn, row : row + 1] = summed[:, :128] + summed[:, 128:]
        part_in[turn, pl.ds(me, 1)] = part_out[pl.ds(turn, 1)]
        each_device(
            lambda to: pltpu.make_async_remote_copy(
                src_ref=part_out.at[turn],
                dst_ref=part_in.at[turn, me],
                send_sem=part_send.at[turn],
                recv_sem=part_recv.at[turn],
                device_id=to,
                device_id_type=MESH,
            ).start()
        )

    def get_sums(turn):
        got = part_in.at[turn, pl.ds(0, devices - 1)]
        pltpu.make_async_copy(got, got, part_recv.at[turn]).wait()
        total = jnp.sum(jnp.sum(part_in[turn], axis=0), axis=1, keepdims=True)
        return total[0:1], total[1:2]

    send_faces(1, residual, packed)
    image, packed = operator(0, residual)

    send_faces(2, image, packed)
    send_sums(0, residual * residual, residual * image)
    second, packed_second = operator(1, image)
    square_0, product = get_sums(0)
    step_0 = square_0 / product
    answer = step_0 * residual
    towards, towards_image, towards_second = residual, image, second
    residual = residual - step_0 * image
    image = image - step_0 * second
    packed = packed - step_0 * packed_second

    send_faces(3, image, packed)
    send_sums(1, residual * residual, residual * image)
    second, _ = operator(2, image)
    square_1, product = get_sums(1)
    ratio = square_1 / square_0
    step_1 = square_1 / (product - ratio * square_1 / step_0)
    towards = residual + ratio * towards
    towards_image = image + ratio * towards_image
    towards_second = second + ratio * towards_second
    answer = answer + step_1 * towards
    residual = residual - step_1 * towards_image
    image = image - step_1 * towards_second

    send_sums(2, residual * residual, residual * image)
    square_2, product = get_sums(2)
    ratio = square_2 / square_1
    step_2 = square_2 / (product - ratio * square_2 / step_1)
    towards = residual + ratio * towards
    towards_image = image + ratio * towards_image
    answer = answer + step_2 * towards
    residual = residual - step_2 * towards_image

    for brick in range(2):
        for x in range(16):
            at = (0, 0, slice(brick, brick + 1), slice(256 * x, 256 * x + 256))
            solution_ref[at] = answer[16 * brick + x : 16 * brick + x + 1]
            residual_ref[at] = residual[16 * brick + x : 16 * brick + x + 1]

    sent = point_out.at[pl.ds(0, wides - 1)]
    pltpu.make_async_copy(sent, sent, point_send.at[0]).wait()
    for turn in range(3):
        sent = part_in.at[turn, pl.ds(0, devices - 1)]
        pltpu.make_async_copy(sent, sent, part_send.at[turn]).wait()
    def wait_sent(a, b, place):
        for turn, source in enumerate(sources):
            sent = source.at[pl.ds(8, 2)]
            pltpu.make_async_copy(sent, sent, halo_send.at[turn, place]).wait()

    each_beside(wait_sent)


def shards(wides, narrows, point_owner, point_cell, normals, strip_count, neighbours):
    points = point_cell.shape[0]
    devices = wides * narrows
    slots = 2 * points // wides
    vmem = pl.BlockSpec(memory_space=pltpu.VMEM)
    hbm = pl.BlockSpec(memory_space=pltpu.HBM)
    smem = pl.BlockSpec(memory_space=pltpu.SMEM)
    out = jax.ShapeDtypeStruct((1, 1, 2, 4096), F32)
    return pl.pallas_call(
        functools.partial(kernel, wides, narrows),
        out_shape=(out, out),
        in_specs=[hbm, hbm, hbm, smem, smem],
        out_specs=(vmem, vmem),
        scratch_shapes=[
            pltpu.VMEM((1, points), jnp.int32),
            pltpu.VMEM((1, points), jnp.int32),
            pltpu.VMEM((3, points), F32),
            pltpu.VMEM((256, 128), BF16),
            pltpu.VMEM((128, 384), BF16),
            pltpu.VMEM((128, 384), BF16),
            pltpu.VMEM((256, 384), BF16),
            pltpu.VMEM((wides, 4, slots), F32),
            pltpu.VMEM((wides, 4, slots), F32),
            pltpu.VMEM((19, 12, 128), F32),
            pltpu.VMEM((19, 12, 128), F32),
            pltpu.VMEM((19, 12, 128), F32),
            pltpu.VMEM((19, 12, 128), F32),
            pltpu.VMEM((3, 2, 128), F32),
            pltpu.VMEM((3, devices, 2, 128), F32),
            pltpu.SemaphoreType.DMA((3,)),
            pltpu.SemaphoreType.DMA((1,)),
            pltpu.SemaphoreType.DMA((1,)),
            pltpu.SemaphoreType.DMA((4, 9)),
            pltpu.SemaphoreType.DMA((4, 9)),
            pltpu.SemaphoreType.DMA((3,)),
            pltpu.SemaphoreType.DMA((3,)),
        ],
        compiler_params=pltpu.CompilerParams(
            collective_id=0, has_side_effects=True, vmem_limit_bytes=32 * 1024 * 1024
        ),
    )(
        point_owner.reshape(1, points), point_cell.reshape(1, points), normals, strip_count, neighbours
    )


def solution(mesh):
    return jax.shard_map(
        functools.partial(shards, mesh.shape["wide"], mesh.shape["narrow"]),
        mesh=mesh,
        in_specs=(
            P(("wide", "narrow"), None),
            P(("wide", "narrow")),
            P(None, ("wide", "narrow")),
            P(("wide", "narrow")),
            P("wide", "narrow", None, None),
        ),
        out_specs=(P("wide", "narrow", None, None), P("wide", "narrow", None, None)),
        check_vma=False,
    )
```

```python
import functools

import jax
import jax.numpy as jnp
from jax import lax
from jax.experimental import pallas as pl
from jax.experimental.pallas import tpu as pltpu
from jax.sharding import PartitionSpec as P

MESH = pl.DeviceIdType.MESH
NT = (((1,), (1,)), ((), ()))
F32 = jnp.float32
BF16 = jnp.bfloat16


def split3(values):
    high = values.astype(BF16).astype(F32)
    rest = values - high
    middle = rest.astype(BF16).astype(F32)
    return high, middle, rest - middle


def one_if(condition):
    return jnp.where(condition, 1.0, 0.0)


def edge(offset):
    return one_if(offset == 0) + 0.5 * one_if((offset == 1) | (offset == -1))


def pack_matrix():
    cell = lax.broadcasted_iota(jnp.int32, (256, 128), 0)
    lane = lax.broadcasted_iota(jnp.int32, (256, 128), 1)
    side, k = (lane // 16) % 4, lane % 16
    wanted = jnp.where(side < 2, k + 240 * side, 16 * k + 15 * (side - 2))
    return one_if(cell == wanted).astype(BF16)


def halo_matrices():
    lane = lax.broadcasted_iota(jnp.int32, (128, 256), 0)
    cell = lax.broadcasted_iota(jnp.int32, (128, 256), 1)
    y, z = cell // 16, cell % 16
    side, k = lane // 16, lane % 16
    face_y = (one_if(side == 0) * one_if(y == 15), one_if(side == 1) * one_if(y == 0))
    face_z = (one_if(side == 2) * one_if(z == 15), one_if(side == 3) * one_if(z == 0))
    corner = (
        one_if((lane == 64) & (y == 15) & (z == 15))
        + one_if((lane == 79) & (y == 15) & (z == 0))
        + one_if((lane == 80) & (y == 0) & (z == 15))
        + one_if((lane == 95) & (y == 0) & (z == 0))
    )
    weight = 0.5 * ((face_y[0] + face_y[1]) * edge(z - k) + (face_z[0] + face_z[1]) * edge(y - k)) + 0.25 * corner
    slope = (face_y[0] - face_y[1]) * one_if(z == k) + (face_z[0] - face_z[1]) * one_if(y == k)
    return weight.astype(BF16), slope.astype(BF16)


def plane_matrix():
    one = lax.broadcasted_iota(jnp.int32, (256, 256), 0)
    two = lax.broadcasted_iota(jnp.int32, (256, 256), 1)
    return (edge(one // 16 - two // 16) * edge(one % 16 - two % 16)).astype(BF16)


def with_packed(matrix, selection):
    return jnp.concatenate([matrix, jnp.dot(matrix, selection, preferred_element_type=F32).astype(BF16)], 1)


def exact_dot(values, matrix):
    rows = values.shape[0]
    parts = jnp.concatenate(split3(values), 0).astype(BF16)
    summed = jnp.dot(parts, matrix, preferred_element_type=F32)
    return summed[:rows] + summed[rows : 2 * rows] + summed[2 * rows :]


def kernel(
    wides, narrows, owner_hbm, cell_hbm, normal_hbm, count_ref, near_ref, solution_ref, residual_ref,
    owner_ref, cell_ref, normal_ref, pack_ref, weight_ref, slope_ref, plane_ref,
    point_out, point_in, vector_src, field_0, field_1, field_2, part_out, part_in,
    in_sem, point_send, point_recv, halo_send, halo_recv, part_send, part_recv,
):
    devices = wides * narrows
    wide = lax.axis_index("wide")
    narrow = lax.axis_index("narrow")
    me = wide * narrows + narrow
    points = cell_ref.shape[1]
    slots = point_out.shape[2]
    loads = [
        pltpu.make_async_copy(source, target, in_sem.at[k])
        for k, (source, target) in enumerate(
            ((owner_hbm, owner_ref), (cell_hbm, cell_ref), (normal_hbm, normal_ref))
        )
    ]
    for load in loads:
        load.start()
    sources = (vector_src, field_0, field_1, field_2)
    for source in sources:
        for place in range(19):
            if place // 2 != 4:
                source[place] = jnp.zeros((12, 128), F32)

    barrier = pltpu.get_barrier_semaphore()

    def after(at, step, count):
        return jnp.where(at + step >= count, at + step - count, at + step)

    def each_device(act):
        if devices > 64:

            @pl.loop(1, devices)
            def _(k):
                other = lax.rem(me + k, devices)
                act((other // narrows, lax.rem(other, narrows)))

            return
        for to_wide in far_first + [wide]:
            for to_narrow in narrow_after[::-1]:
                if to_wide is not wide or to_narrow is not narrow:
                    act((to_wide, to_narrow))

    far_first = []
    if wides & (wides - 1):
        far_first = [after(wide, k, wides) for k in range(1, wides)]
    else:
        flips = []
        bit = 1
        while bit < wides:
            flips.append((1 - 2 * (lax.div(wide, bit) % 2)) * bit)
            bit = 2 * bit
        for k in range(wides - 1, 0, -1):
            far_first.append(wide + sum(flip for j, flip in enumerate(flips) if k >> j & 1))
    narrow_after = [narrow] + [after(narrow, k, narrows) for k in range(1, narrows)]
    each_device(lambda to: pl.semaphore_signal(barrier, inc=1, device_id=to, device_id_type=MESH))

    if narrows == 2:
        turns = (1 - 2 * narrow,)
    else:
        turns = (-1, 1)
    groups = []
    for a in (1, -1):
        there = (wide + a >= 0) & (wide + a < wides)
        if narrows == 2:
            groups.append((there, [(a, turns[0]), (a, 0)]))
        else:
            groups.append((there, [(a, 0)]))
            for b in turns:
                groups.append((there & (narrow + b >= 0) & (narrow + b < narrows), [(a, b)]))
    for b in turns:
        groups.append((None if narrows == 2 else (narrow + b >= 0) & (narrow + b < narrows), [(0, b)]))

    def each_beside(act):
        for there, peers in groups:

            def body(peers=peers):
                for a, b in peers:
                    act(a, b, (a + 1) * 3 + b + 1)

            if there is None:
                body()
            else:
                pl.when(there)(body)

    for load in loads:
        load.wait()

    owner = owner_ref[...]
    live = lax.broadcasted_iota(jnp.int32, (1, points), 1) < count_ref[0]
    owned = lax.broadcasted_iota(jnp.int32, (wides, points), 0) == owner
    owner_hot = one_if(owned)
    blocks = points // 128
    stacked = jnp.concatenate([owner_hot[:, k * 128 : (k + 1) * 128] for k in range(blocks)], 0)
    earlier = jnp.where(
        lax.broadcasted_iota(jnp.int32, (128, 256), 0) < lax.broadcasted_iota(jnp.int32, (128, 256), 1),
        1.0,
        0.0,
    )
    counted = jnp.dot(stacked.astype(BF16), earlier.astype(BF16), preferred_element_type=F32)
    ranks = []
    before = jnp.zeros((wides, 128), F32)
    for k in range(blocks):
        rows = slice(k * wides, (k + 1) * wides)
        ranks.append(
            jnp.sum(stacked[rows] * (counted[rows, :128] + before), axis=0, keepdims=True)
        )
        before = before + counted[rows, 128:]
    rank = jnp.concatenate(ranks, 1).astype(jnp.int32)
    code = jnp.where(live, cell_ref[...] + 1, 0)
    rows = [lax.shift_right_logical(code, 8).astype(F32), (code & 255).astype(F32)]
    for c in range(3):
        rows.extend(split3(normal_ref[c : c + 1]))
    weighted = jnp.concatenate([jnp.where(owned, row, 0.0) for row in rows], 0).astype(BF16)
    rank_hot = one_if(lax.broadcasted_iota(jnp.int32, (slots, points), 0) == rank).astype(BF16)
    moved = lax.dot_general(weighted, rank_hot, NT, preferred_element_type=F32)
    moved = [moved[k * wides : (k + 1) * wides] for k in range(11)]
    values = [moved[2 + 3 * c] + moved[3 + 3 * c] + moved[4 + 3 * c] for c in range(3)]
    values.append(256.0 * moved[0] + moved[1])
    for k in range(wides):
        for c in range(4):
            point_out[k, c : c + 1] = values[c][k : k + 1]

    pl.semaphore_wait(barrier, devices - 1)

    for other in far_first:
        pltpu.make_async_remote_copy(
            src_ref=point_out.at[other],
            dst_ref=point_in.at[wide],
            send_sem=point_send.at[0],
            recv_sem=point_recv.at[0],
            device_id=(other, narrow),
            device_id_type=MESH,
        ).start()

    pack_ref[...] = pack_matrix()
    weight, slope = halo_matrices()
    weight_ref[...] = with_packed(weight, pack_ref[...])
    slope_ref[...] = with_packed(slope, pack_ref[...])
    plane_ref[...] = with_packed(plane_matrix(), pack_ref[...])
    point_in[pl.ds(wide, 1)] = point_out[pl.ds(wide, 1)]
    arrived = point_in.at[pl.ds(0, wides - 1)]
    pltpu.make_async_copy(arrived, arrived, point_recv.at[0]).wait()

    group = 8 if slots % 128 == 0 and wides % 8 == 0 else 1
    splatted = jnp.zeros((320, 256), F32)
    for k in range(0, wides, group):
        got = jnp.concatenate([point_in[k + j] for j in range(group)], 1)
        width = group * slots
        cell = got[3:4].astype(jnp.int32) - 1
        row_hot = lax.broadcasted_iota(jnp.int32, (32, width), 0) == lax.shift_right_arithmetic(cell, 8)
        lane_hot = lax.broadcasted_iota(jnp.int32, (256, width), 0) == (cell & 255)
        weights = []
        for c in range(3):
            weights.extend(split3(got[c : c + 1]))
        weights.append(jnp.ones((1, width), F32))
        weighted = jnp.concatenate([jnp.where(row_hot, w, 0.0) for w in weights], 0).astype(BF16)
        splatted = splatted + lax.dot_general(
            weighted, jnp.where(lane_hot, 1.0, 0.0).astype(BF16), NT, preferred_element_type=F32
        )
    vectors = [
        splatted[96 * c : 96 * c + 32] + splatted[96 * c + 32 : 96 * c + 64] + splatted[96 * c + 64 : 96 * c + 96]
        for c in range(3)
    ]
    shifted_diagonal = 16.5 + 2.0 * splatted[288:320]

    def halo_start(source, turn):
        def start(a, b, place):
            pltpu.make_async_remote_copy(
                src_ref=source.at[pl.ds(8, 2)],
                dst_ref=source.at[pl.ds(2 * (8 - place), 2)],
                send_sem=halo_send.at[turn, place],
                recv_sem=halo_recv.at[turn, 8 - place],
                device_id=(wide + a, narrow + b),
                device_id_type=MESH,
            ).start()

        each_beside(start)

    def halo_wait(source, turn):
        def wait(a, b, place):
            got = source.at[pl.ds(2 * place, 2)]
            pltpu.make_async_copy(got, got, halo_recv.at[turn, place]).wait()

        each_beside(wait)

    def near(brick, a, b, c):
        return near_ref[0, 0, brick, (a + 1) * 9 + (b + 1) * 3 + c + 1]

    cell_at = lax.broadcasted_iota(jnp.int32, (32, 256), 1)
    x_at = lax.broadcasted_iota(jnp.int32, (32, 256), 0) % 16
    y_at, z_at = cell_at // 16, cell_at % 16
    low_half = lax.broadcasted_iota(jnp.int32, (8, 128), 1) < 64

    def send_faces(turn, ends, packed):
        source = sources[turn]
        for brick in range(2):
            row = 16 * brick
            source[8 + brick, 0:8] = jnp.where(low_half, packed[row : row + 8], packed[row + 8 : row + 16])
            for k, x in enumerate((0, 15)):
                for half in range(2):
                    at = 8 + 2 * k + half
                    source[8 + brick, at : at + 1] = ends[row + x : row + x + 1, 128 * half : 128 * half + 128]
        halo_start(source, turn)

    def ends_of(source):
        rows = []
        for brick in range(2):
            low, high = near(brick, -1, 0, 0), near(brick, 1, 0, 0)
            rows.append(jnp.concatenate([source[low, 10:11, :], source[low, 11:12, :]], 1))
            rows.append(jnp.concatenate([source[high, 8:9, :], source[high, 9:10, :]], 1))
        return jnp.concatenate(rows + [jnp.zeros((4, 256), F32)], 0)

    x_wide = lax.broadcasted_iota(jnp.int32, (16, 384), 0)

    def at_ends(rows, sign):
        return jnp.concatenate(
            [
                jnp.where(
                    x_wide == 0, sign * rows[2 * k : 2 * k + 1], jnp.where(x_wide == 15, rows[2 * k + 1 : 2 * k + 2], 0.0)
                )
                for k in range(2)
            ],
            0,
        )

    def pack(values):
        return exact_dot(values, pack_ref[...])

    def merged(source, brick, a, rows, corners):
        lane = lax.broadcasted_iota(jnp.int32, (rows.stop - rows.start, 128), 1) % 64

        def beside(b, c):
            return source[near(brick, a, b, c), rows, :]

        faces = jnp.where(
            lane < 32,
            jnp.where(lane < 16, beside(1, 0), beside(-1, 0)),
            jnp.where(lane < 48, beside(0, 1), beside(0, -1)),
        )
        if not corners:
            return faces, faces
        corner = jnp.where(
            lane < 16,
            jnp.where(lane == 0, beside(1, 1), beside(1, -1)),
            jnp.where(lane == 16, beside(-1, 1), beside(-1, -1)),
        )
        return faces, corner

    def swap(values):
        return pltpu.roll(values, 64, 1)

    def faces_of(source, brick, corners):
        faces, corner = merged(source, brick, 0, slice(0, 8), corners)
        return jnp.concatenate(
            [jnp.where(low_half, faces, swap(corner)), jnp.where(low_half, swap(faces), corner)], 0
        )

    send_faces(
        0,
        vectors[0],
        jnp.where(
            lax.broadcasted_iota(jnp.int32, (32, 128), 1) % 64 < 32,
            exact_dot(vectors[1], pack_ref[...]),
            exact_dot(vectors[2], pack_ref[...]),
        ),
    )
    change = (
        jnp.where(x_at == 15, 0.0, pltpu.roll(vectors[0], 31, 0))
        - jnp.where(x_at == 0, 0.0, pltpu.roll(vectors[0], 1, 0))
        + jnp.where(y_at == 15, 0.0, pltpu.roll(vectors[1], 240, 1))
        - jnp.where(y_at == 0, 0.0, pltpu.roll(vectors[1], 16, 1))
        + jnp.where(z_at == 15, 0.0, pltpu.roll(vectors[2], 255, 1))
        - jnp.where(z_at == 0, 0.0, pltpu.roll(vectors[2], 1, 1))
    )
    change = jnp.concatenate([change, pack(change)], 1)
    halo_wait(vector_src, 0)
    ends = ends_of(vector_src)
    faces = jnp.concatenate([faces_of(vector_src, brick, False) for brick in range(2)], 0)
    change = (
        change
        + at_ends(jnp.concatenate([ends, pack(ends)], 1), -1.0)
        + exact_dot(faces, slope_ref[...])
    )
    change = -4.0 * change
    residual, packed = change[:, :256], change[:, 256:]

    def plane_sum(values):
        summed = values + 0.5 * (
            jnp.where(z_at == 0, 0.0, pltpu.roll(values, 1, 1))
            + jnp.where(z_at == 15, 0.0, pltpu.roll(values, 255, 1))
        )
        return summed + 0.5 * (
            jnp.where(y_at == 0, 0.0, pltpu.roll(summed, 16, 1))
            + jnp.where(y_at == 15, 0.0, pltpu.roll(summed, 240, 1))
        )

    def operator(turn, values):
        source = sources[1 + turn]
        inner = values + 0.5 * (
            jnp.where(x_at == 0, 0.0, pltpu.roll(values, 1, 0))
            + jnp.where(x_at == 15, 0.0, pltpu.roll(values, 31, 0))
        )
        own = shifted_diagonal * values - 2.0 * plane_sum(inner)
        own = jnp.concatenate([own, pack(own)], 1)
        halo_wait(source, 1 + turn)
        ends = at_ends(exact_dot(ends_of(source), plane_ref[...]), 1.0)
        row_at = lax.broadcasted_iota(jnp.int32, (16, 128), 0)
        half_row = lax.broadcasted_iota(jnp.int32, (1, 128), 1) < 64
        faces = []
        for brick in range(2):
            here = faces_of(source, brick, True)
            face, corner = merged(source, brick, -1, slice(7, 8), True)
            low = jnp.where(half_row, swap(face), corner)
            face, corner = merged(source, brick, 1, slice(0, 1), True)
            high = jnp.where(half_row, face, swap(corner))
            faces.append(
                here
                + 0.5
                * (
                    jnp.where(row_at == 0, low, pltpu.roll(here, 1, 0))
                    + jnp.where(row_at == 15, high, pltpu.roll(here, 15, 0))
                )
            )
        both = own - ends - 2.0 * exact_dot(jnp.concatenate(faces, 0), weight_ref[...])
        return both[:, :256], both[:, 256:]

    def send_sums(turn, one, two):
        for row, values in enumerate((one, two)):
            summed = jnp.sum(values, axis=0, keepdims=True)
            part_out[turn, row : row + 1] = summed[:, :128] + summed[:, 128:]
        part_in[turn, pl.ds(me, 1)] = part_out[pl.ds(turn, 1)]
        each_device(
            lambda to: pltpu.make_async_remote_copy(
                src_ref=part_out.at[turn],
                dst_ref=part_in.at[turn, me],
                send_sem=part_send.at[turn],
                recv_sem=part_recv.at[turn],
                device_id=to,
                device_id_type=MESH,
            ).start()
        )

    def get_sums(turn):
        got = part_in.at[turn, pl.ds(0, devices - 1)]
        pltpu.make_async_copy(got, got, part_recv.at[turn]).wait()
        total = jnp.sum(jnp.sum(part_in[turn], axis=0), axis=1, keepdims=True)
        return total[0:1], total[1:2]

    send_faces(1, residual, packed)
    image, packed = operator(0, residual)

    send_faces(2, image, packed)
    send_sums(0, residual * residual, residual * image)
    second, packed_second = operator(1, image)
    square_0, product = get_sums(0)
    step_0 = square_0 / product
    answer = step_0 * residual
    towards, towards_image, towards_second = residual, image, second
    residual = residual - step_0 * image
    image = image - step_0 * second
    packed = packed - step_0 * packed_second

    send_faces(3, image, packed)
    send_sums(1, residual * residual, residual * image)
    second, _ = operator(2, image)
    square_1, product = get_sums(1)
    ratio = square_1 / square_0
    step_1 = square_1 / (product - ratio * square_1 / step_0)
    towards = residual + ratio * towards
    towards_image = image + ratio * towards_image
    towards_second = second + ratio * towards_second
    answer = answer + step_1 * towards
    residual = residual - step_1 * towards_image
    image = image - step_1 * towards_second

    send_sums(2, residual * residual, residual * image)
    square_2, product = get_sums(2)
    ratio = square_2 / square_1
    step_2 = square_2 / (product - ratio * square_2 / step_1)
    towards = residual + ratio * towards
    towards_image = image + ratio * towards_image
    answer = answer + step_2 * towards
    residual = residual - step_2 * towards_image

    for brick in range(2):
        for x in range(16):
            at = (0, 0, slice(brick, brick + 1), slice(256 * x, 256 * x + 256))
            solution_ref[at] = answer[16 * brick + x : 16 * brick + x + 1]
            residual_ref[at] = residual[16 * brick + x : 16 * brick + x + 1]

    sent = point_out.at[pl.ds(0, wides - 1)]
    pltpu.make_async_copy(sent, sent, point_send.at[0]).wait()
    for turn in range(3):
        sent = part_in.at[turn, pl.ds(0, devices - 1)]
        pltpu.make_async_copy(sent, sent, part_send.at[turn]).wait()
    def wait_sent(a, b, place):
        for turn, source in enumerate(sources):
            sent = source.at[pl.ds(8, 2)]
            pltpu.make_async_copy(sent, sent, halo_send.at[turn, place]).wait()

    each_beside(wait_sent)


def shards(wides, narrows, point_owner, point_cell, normals, strip_count, neighbours):
    points = point_cell.shape[0]
    devices = wides * narrows
    slots = 2 * points // wides
    vmem = pl.BlockSpec(memory_space=pltpu.VMEM)
    hbm = pl.BlockSpec(memory_space=pltpu.HBM)
    smem = pl.BlockSpec(memory_space=pltpu.SMEM)
    out = jax.ShapeDtypeStruct((1, 1, 2, 4096), F32)
    return pl.pallas_call(
        functools.partial(kernel, wides, narrows),
        out_shape=(out, out),
        in_specs=[hbm, hbm, hbm, smem, smem],
        out_specs=(vmem, vmem),
        scratch_shapes=[
            pltpu.VMEM((1, points), jnp.int32),
            pltpu.VMEM((1, points), jnp.int32),
            pltpu.VMEM((3, points), F32),
            pltpu.VMEM((256, 128), BF16),
            pltpu.VMEM((128, 384), BF16),
            pltpu.VMEM((128, 384), BF16),
            pltpu.VMEM((256, 384), BF16),
            pltpu.VMEM((wides, 4, slots), F32),
            pltpu.VMEM((wides, 4, slots), F32),
            pltpu.VMEM((19, 12, 128), F32),
            pltpu.VMEM((19, 12, 128), F32),
            pltpu.VMEM((19, 12, 128), F32),
            pltpu.VMEM((19, 12, 128), F32),
            pltpu.VMEM((3, 2, 128), F32),
            pltpu.VMEM((3, devices, 2, 128), F32),
            pltpu.SemaphoreType.DMA((3,)),
            pltpu.SemaphoreType.DMA((1,)),
            pltpu.SemaphoreType.DMA((1,)),
            pltpu.SemaphoreType.DMA((4, 9)),
            pltpu.SemaphoreType.DMA((4, 9)),
            pltpu.SemaphoreType.DMA((3,)),
            pltpu.SemaphoreType.DMA((3,)),
        ],
        compiler_params=pltpu.CompilerParams(
            collective_id=0, has_side_effects=True, vmem_limit_bytes=56 * 1024 * 1024
        ),
    )(
        point_owner.reshape(1, points), point_cell.reshape(1, points), normals, strip_count, neighbours
    )


def solution(mesh):
    return jax.shard_map(
        functools.partial(shards, mesh.shape["wide"], mesh.shape["narrow"]),
        mesh=mesh,
        in_specs=(
            P(("wide", "narrow"), None),
            P(("wide", "narrow")),
            P(None, ("wide", "narrow")),
            P(("wide", "narrow")),
            P("wide", "narrow", None, None),
        ),
        out_specs=(P("wide", "narrow", None, None), P("wide", "narrow", None, None)),
        check_vma=False,
    )
```

```python
import functools

import jax
import jax.numpy as jnp
from jax import lax
from jax.experimental import pallas as pl
from jax.experimental.pallas import tpu as pltpu
from jax.sharding import PartitionSpec as P

MESH = pl.DeviceIdType.MESH
NT = (((1,), (1,)), ((), ()))
F32 = jnp.float32
BF16 = jnp.bfloat16


def split3(values):
    high = values.astype(BF16).astype(F32)
    rest = values - high
    middle = rest.astype(BF16).astype(F32)
    return high, middle, rest - middle


def one_if(condition):
    return jnp.where(condition, 1.0, 0.0)


def edge(offset):
    return one_if(offset == 0) + 0.5 * one_if((offset == 1) | (offset == -1))


def pack_matrix():
    cell = lax.broadcasted_iota(jnp.int32, (256, 128), 0)
    lane = lax.broadcasted_iota(jnp.int32, (256, 128), 1)
    side, k = (lane // 16) % 4, lane % 16
    wanted = jnp.where(side < 2, k + 240 * side, 16 * k + 15 * (side - 2))
    return one_if(cell == wanted).astype(BF16)


def halo_matrices():
    lane = lax.broadcasted_iota(jnp.int32, (128, 256), 0)
    cell = lax.broadcasted_iota(jnp.int32, (128, 256), 1)
    y, z = cell // 16, cell % 16
    side, k = lane // 16, lane % 16
    face_y = (one_if(side == 0) * one_if(y == 15), one_if(side == 1) * one_if(y == 0))
    face_z = (one_if(side == 2) * one_if(z == 15), one_if(side == 3) * one_if(z == 0))
    corner = (
        one_if((lane == 64) & (y == 15) & (z == 15))
        + one_if((lane == 79) & (y == 15) & (z == 0))
        + one_if((lane == 80) & (y == 0) & (z == 15))
        + one_if((lane == 95) & (y == 0) & (z == 0))
    )
    weight = 0.5 * ((face_y[0] + face_y[1]) * edge(z - k) + (face_z[0] + face_z[1]) * edge(y - k)) + 0.25 * corner
    slope = (face_y[0] - face_y[1]) * one_if(z == k) + (face_z[0] - face_z[1]) * one_if(y == k)
    return weight.astype(BF16), slope.astype(BF16)


def plane_matrix():
    one = lax.broadcasted_iota(jnp.int32, (256, 256), 0)
    two = lax.broadcasted_iota(jnp.int32, (256, 256), 1)
    return (edge(one // 16 - two // 16) * edge(one % 16 - two % 16)).astype(BF16)


def with_packed(matrix, selection):
    return jnp.concatenate([matrix, jnp.dot(matrix, selection, preferred_element_type=F32).astype(BF16)], 1)


def exact_dot(values, matrix):
    rows = values.shape[0]
    parts = jnp.concatenate(split3(values), 0).astype(BF16)
    summed = jnp.dot(parts, matrix, preferred_element_type=F32)
    return summed[:rows] + summed[rows : 2 * rows] + summed[2 * rows :]


def kernel(
    wides, narrows, owner_hbm, cell_hbm, normal_hbm, count_ref, near_ref, solution_ref, residual_ref,
    owner_ref, cell_ref, normal_ref, pack_ref, weight_ref, slope_ref, plane_ref,
    point_out, point_in, vector_src, field_0, field_1, field_2, part_out, part_in,
    in_sem, point_send, point_recv, halo_send, halo_recv, part_send, part_recv,
):
    devices = wides * narrows
    wide = lax.axis_index("wide")
    narrow = lax.axis_index("narrow")
    me = wide * narrows + narrow
    points = cell_ref.shape[1]
    slots = point_out.shape[2]
    loads = [
        pltpu.make_async_copy(source, target, in_sem.at[k])
        for k, (source, target) in enumerate(
            ((owner_hbm, owner_ref), (cell_hbm, cell_ref), (normal_hbm, normal_ref))
        )
    ]
    for load in loads:
        load.start()
    sources = (vector_src, field_0, field_1, field_2)
    for source in sources:
        for place in range(19):
            if place // 2 != 4:
                source[place] = jnp.zeros((12, 128), F32)

    barrier = pltpu.get_barrier_semaphore()

    def after(at, step, count):
        return jnp.where(at + step >= count, at + step - count, at + step)

    def each_device(act):
        if devices > 64:

            @pl.loop(1, devices)
            def _(k):
                other = lax.rem(me + k, devices)
                act((other // narrows, lax.rem(other, narrows)))

            return
        for to_wide in far_first + [wide]:
            for to_narrow in narrow_after[::-1]:
                if to_wide is not wide or to_narrow is not narrow:
                    act((to_wide, to_narrow))

    far_first = []
    if wides & (wides - 1):
        far_first = [after(wide, k, wides) for k in range(1, wides)]
    else:
        flips = []
        bit = 1
        while bit < wides:
            flips.append((1 - 2 * (lax.div(wide, bit) % 2)) * bit)
            bit = 2 * bit
        for k in range(wides - 1, 0, -1):
            far_first.append(wide + sum(flip for j, flip in enumerate(flips) if k >> j & 1))
    narrow_after = [narrow] + [after(narrow, k, narrows) for k in range(1, narrows)]
    each_device(lambda to: pl.semaphore_signal(barrier, inc=1, device_id=to, device_id_type=MESH))

    if narrows == 2:
        turns = (1 - 2 * narrow,)
    else:
        turns = (-1, 1)
    groups = []
    for a in (1, -1):
        there = (wide + a >= 0) & (wide + a < wides)
        if narrows == 2:
            groups.append((there, [(a, turns[0]), (a, 0)]))
        else:
            groups.append((there, [(a, 0)]))
            for b in turns:
                groups.append((there & (narrow + b >= 0) & (narrow + b < narrows), [(a, b)]))
    for b in turns:
        groups.append((None if narrows == 2 else (narrow + b >= 0) & (narrow + b < narrows), [(0, b)]))

    def each_beside(act):
        for there, peers in groups:

            def body(peers=peers):
                for a, b in peers:
                    act(a, b, (a + 1) * 3 + b + 1)

            if there is None:
                body()
            else:
                pl.when(there)(body)

    for load in loads:
        load.wait()

    owner = owner_ref[...]
    live = lax.broadcasted_iota(jnp.int32, (1, points), 1) < count_ref[0]
    owned = lax.broadcasted_iota(jnp.int32, (wides, points), 0) == owner
    owner_hot = one_if(owned)
    blocks = points // 128
    stacked = jnp.concatenate([owner_hot[:, k * 128 : (k + 1) * 128] for k in range(blocks)], 0)
    earlier = jnp.where(
        lax.broadcasted_iota(jnp.int32, (128, 256), 0) < lax.broadcasted_iota(jnp.int32, (128, 256), 1),
        1.0,
        0.0,
    )
    counted = jnp.dot(stacked.astype(BF16), earlier.astype(BF16), preferred_element_type=F32)
    ranks = []
    before = jnp.zeros((wides, 128), F32)
    for k in range(blocks):
        rows = slice(k * wides, (k + 1) * wides)
        ranks.append(
            jnp.sum(stacked[rows] * (counted[rows, :128] + before), axis=0, keepdims=True)
        )
        before = before + counted[rows, 128:]
    rank = jnp.concatenate(ranks, 1).astype(jnp.int32)
    code = jnp.where(live, cell_ref[...] + 1, 0)
    rows = [lax.shift_right_logical(code, 8).astype(F32), (code & 255).astype(F32)]
    for c in range(3):
        rows.extend(split3(normal_ref[c : c + 1]))
    weighted = jnp.concatenate([jnp.where(owned, row, 0.0) for row in rows], 0).astype(BF16)
    rank_hot = one_if(lax.broadcasted_iota(jnp.int32, (slots, points), 0) == rank).astype(BF16)
    moved = lax.dot_general(weighted, rank_hot, NT, preferred_element_type=F32)
    moved = [moved[k * wides : (k + 1) * wides] for k in range(11)]
    values = [moved[2 + 3 * c] + moved[3 + 3 * c] + moved[4 + 3 * c] for c in range(3)]
    values.append(256.0 * moved[0] + moved[1])
    for k in range(wides):
        for c in range(4):
            point_out[k, c : c + 1] = values[c][k : k + 1]

    pl.semaphore_wait(barrier, devices - 1)

    for other in far_first:
        pltpu.make_async_remote_copy(
            src_ref=point_out.at[other],
            dst_ref=point_in.at[wide],
            send_sem=point_send.at[0],
            recv_sem=point_recv.at[0],
            device_id=(other, narrow),
            device_id_type=MESH,
        ).start()

    pack_ref[...] = pack_matrix()
    weight, slope = halo_matrices()
    weight_ref[...] = with_packed(weight, pack_ref[...])
    slope_ref[...] = with_packed(slope, pack_ref[...])
    plane_ref[...] = with_packed(plane_matrix(), pack_ref[...])
    point_in[pl.ds(wide, 1)] = point_out[pl.ds(wide, 1)]
    arrived = point_in.at[pl.ds(0, wides - 1)]
    pltpu.make_async_copy(arrived, arrived, point_recv.at[0]).wait()

    group = 8 if slots % 128 == 0 and wides % 8 == 0 else 1
    splatted = jnp.zeros((320, 256), F32)
    for k in range(0, wides, group):
        got = jnp.concatenate([point_in[k + j] for j in range(group)], 1)
        width = group * slots
        cell = got[3:4].astype(jnp.int32) - 1
        row_hot = lax.broadcasted_iota(jnp.int32, (32, width), 0) == lax.shift_right_arithmetic(cell, 8)
        lane_hot = lax.broadcasted_iota(jnp.int32, (256, width), 0) == (cell & 255)
        weights = []
        for c in range(3):
            weights.extend(split3(got[c : c + 1]))
        weights.append(jnp.ones((1, width), F32))
        weighted = jnp.concatenate([jnp.where(row_hot, w, 0.0) for w in weights], 0).astype(BF16)
        splatted = splatted + lax.dot_general(
            weighted, jnp.where(lane_hot, 1.0, 0.0).astype(BF16), NT, preferred_element_type=F32
        )
    vectors = [
        splatted[96 * c : 96 * c + 32] + splatted[96 * c + 32 : 96 * c + 64] + splatted[96 * c + 64 : 96 * c + 96]
        for c in range(3)
    ]
    shifted_diagonal = 16.5 + 2.0 * splatted[288:320]

    def halo_start(source, turn):
        def start(a, b, place):
            pltpu.make_async_remote_copy(
                src_ref=source.at[pl.ds(8, 2)],
                dst_ref=source.at[pl.ds(2 * (8 - place), 2)],
                send_sem=halo_send.at[turn, place],
                recv_sem=halo_recv.at[turn, 8 - place],
                device_id=(wide + a, narrow + b),
                device_id_type=MESH,
            ).start()

        each_beside(start)

    def halo_wait(source, turn):
        def wait(a, b, place):
            got = source.at[pl.ds(2 * place, 2)]
            pltpu.make_async_copy(got, got, halo_recv.at[turn, place]).wait()

        each_beside(wait)

    def near(brick, a, b, c):
        return near_ref[0, 0, brick, (a + 1) * 9 + (b + 1) * 3 + c + 1]

    cell_at = lax.broadcasted_iota(jnp.int32, (32, 256), 1)
    x_at = lax.broadcasted_iota(jnp.int32, (32, 256), 0) % 16
    y_at, z_at = cell_at // 16, cell_at % 16
    low_half = lax.broadcasted_iota(jnp.int32, (8, 128), 1) < 64

    def send_faces(turn, ends, packed):
        source = sources[turn]
        for brick in range(2):
            row = 16 * brick
            source[8 + brick, 0:8] = jnp.where(low_half, packed[row : row + 8], packed[row + 8 : row + 16])
            for k, x in enumerate((0, 15)):
                for half in range(2):
                    at = 8 + 2 * k + half
                    source[8 + brick, at : at + 1] = ends[row + x : row + x + 1, 128 * half : 128 * half + 128]
        halo_start(source, turn)

    def ends_of(source):
        rows = []
        for brick in range(2):
            low, high = near(brick, -1, 0, 0), near(brick, 1, 0, 0)
            rows.append(jnp.concatenate([source[low, 10:11, :], source[low, 11:12, :]], 1))
            rows.append(jnp.concatenate([source[high, 8:9, :], source[high, 9:10, :]], 1))
        return jnp.concatenate(rows + [jnp.zeros((4, 256), F32)], 0)

    x_wide = lax.broadcasted_iota(jnp.int32, (16, 384), 0)

    def at_ends(rows, sign):
        return jnp.concatenate(
            [
                jnp.where(
                    x_wide == 0, sign * rows[2 * k : 2 * k + 1], jnp.where(x_wide == 15, rows[2 * k + 1 : 2 * k + 2], 0.0)
                )
                for k in range(2)
            ],
            0,
        )

    def pack(values):
        return exact_dot(values, pack_ref[...])

    def merged(source, brick, a, rows, corners):
        lane = lax.broadcasted_iota(jnp.int32, (rows.stop - rows.start, 128), 1) % 64

        def beside(b, c):
            return source[near(brick, a, b, c), rows, :]

        faces = jnp.where(
            lane < 32,
            jnp.where(lane < 16, beside(1, 0), beside(-1, 0)),
            jnp.where(lane < 48, beside(0, 1), beside(0, -1)),
        )
        if not corners:
            return faces, faces
        corner = jnp.where(
            lane < 16,
            jnp.where(lane == 0, beside(1, 1), beside(1, -1)),
            jnp.where(lane == 16, beside(-1, 1), beside(-1, -1)),
        )
        return faces, corner

    def swap(values):
        return pltpu.roll(values, 64, 1)

    def faces_of(source, brick, corners):
        faces, corner = merged(source, brick, 0, slice(0, 8), corners)
        return jnp.concatenate(
            [jnp.where(low_half, faces, swap(corner)), jnp.where(low_half, swap(faces), corner)], 0
        )

    send_faces(
        0,
        vectors[0],
        jnp.where(
            lax.broadcasted_iota(jnp.int32, (32, 128), 1) % 64 < 32,
            exact_dot(vectors[1], pack_ref[...]),
            exact_dot(vectors[2], pack_ref[...]),
        ),
    )
    change = (
        jnp.where(x_at == 15, 0.0, pltpu.roll(vectors[0], 31, 0))
        - jnp.where(x_at == 0, 0.0, pltpu.roll(vectors[0], 1, 0))
        + jnp.where(y_at == 15, 0.0, pltpu.roll(vectors[1], 240, 1))
        - jnp.where(y_at == 0, 0.0, pltpu.roll(vectors[1], 16, 1))
        + jnp.where(z_at == 15, 0.0, pltpu.roll(vectors[2], 255, 1))
        - jnp.where(z_at == 0, 0.0, pltpu.roll(vectors[2], 1, 1))
    )
    change = jnp.concatenate([change, pack(change)], 1)
    halo_wait(vector_src, 0)
    ends = ends_of(vector_src)
    faces = jnp.concatenate([faces_of(vector_src, brick, False) for brick in range(2)], 0)
    change = (
        change
        + at_ends(jnp.concatenate([ends, pack(ends)], 1), -1.0)
        + exact_dot(faces, slope_ref[...])
    )
    change = -4.0 * change
    residual, packed = change[:, :256], change[:, 256:]

    def plane_sum(values):
        summed = values + 0.5 * (
            jnp.where(z_at == 0, 0.0, pltpu.roll(values, 1, 1))
            + jnp.where(z_at == 15, 0.0, pltpu.roll(values, 255, 1))
        )
        return summed + 0.5 * (
            jnp.where(y_at == 0, 0.0, pltpu.roll(summed, 16, 1))
            + jnp.where(y_at == 15, 0.0, pltpu.roll(summed, 240, 1))
        )

    def operator(turn, values):
        source = sources[1 + turn]
        inner = values + 0.5 * (
            jnp.where(x_at == 0, 0.0, pltpu.roll(values, 1, 0))
            + jnp.where(x_at == 15, 0.0, pltpu.roll(values, 31, 0))
        )
        own = shifted_diagonal * values - 2.0 * plane_sum(inner)
        own = jnp.concatenate([own, pack(own)], 1)
        halo_wait(source, 1 + turn)
        ends = at_ends(exact_dot(ends_of(source), plane_ref[...]), 1.0)
        row_at = lax.broadcasted_iota(jnp.int32, (16, 128), 0)
        half_row = lax.broadcasted_iota(jnp.int32, (1, 128), 1) < 64
        faces = []
        for brick in range(2):
            here = faces_of(source, brick, True)
            face, corner = merged(source, brick, -1, slice(7, 8), True)
            low = jnp.where(half_row, swap(face), corner)
            face, corner = merged(source, brick, 1, slice(0, 1), True)
            high = jnp.where(half_row, face, swap(corner))
            faces.append(
                here
                + 0.5
                * (
                    jnp.where(row_at == 0, low, pltpu.roll(here, 1, 0))
                    + jnp.where(row_at == 15, high, pltpu.roll(here, 15, 0))
                )
            )
        both = own - ends - 2.0 * exact_dot(jnp.concatenate(faces, 0), weight_ref[...])
        return both[:, :256], both[:, 256:]

    def send_sums(turn, one, two):
        for row, values in enumerate((one, two)):
            summed = jnp.sum(values, axis=0, keepdims=True)
            part_out[turn, row : row + 1] = summed[:, :128] + summed[:, 128:]
        part_in[turn, pl.ds(me, 1)] = part_out[pl.ds(turn, 1)]
        each_device(
            lambda to: pltpu.make_async_remote_copy(
                src_ref=part_out.at[turn],
                dst_ref=part_in.at[turn, me],
                send_sem=part_send.at[turn],
                recv_sem=part_recv.at[turn],
                device_id=to,
                device_id_type=MESH,
            ).start()
        )

    def get_sums(turn):
        got = part_in.at[turn, pl.ds(0, devices - 1)]
        pltpu.make_async_copy(got, got, part_recv.at[turn]).wait()
        total = jnp.sum(jnp.sum(part_in[turn], axis=0), axis=1, keepdims=True)
        return total[0:1], total[1:2]

    send_faces(1, residual, packed)
    image, packed = operator(0, residual)

    send_faces(2, image, packed)
    send_sums(0, residual * residual, residual * image)
    second, packed_second = operator(1, image)
    square_0, product = get_sums(0)
    step_0 = square_0 / product
    answer = step_0 * residual
    towards, towards_image, towards_second = residual, image, second
    residual = residual - step_0 * image
    image = image - step_0 * second
    packed = packed - step_0 * packed_second

    send_faces(3, image, packed)
    send_sums(1, residual * residual, residual * image)
    second, _ = operator(2, image)
    square_1, product = get_sums(1)
    ratio = square_1 / square_0
    step_1 = square_1 / (product - ratio * square_1 / step_0)
    towards = residual + ratio * towards
    towards_image = image + ratio * towards_image
    towards_second = second + ratio * towards_second
    answer = answer + step_1 * towards
    residual = residual - step_1 * towards_image
    image = image - step_1 * towards_second

    send_sums(2, residual * residual, residual * image)
    square_2, product = get_sums(2)
    ratio = square_2 / square_1
    step_2 = square_2 / (product - ratio * square_2 / step_1)
    towards = residual + ratio * towards
    towards_image = image + ratio * towards_image
    answer = answer + step_2 * towards
    residual = residual - step_2 * towards_image

    for brick in range(2):
        for x in range(16):
            at = (0, 0, slice(brick, brick + 1), slice(256 * x, 256 * x + 256))
            solution_ref[at] = answer[16 * brick + x : 16 * brick + x + 1]
            residual_ref[at] = residual[16 * brick + x : 16 * brick + x + 1]

    sent = point_out.at[pl.ds(0, wides - 1)]
    pltpu.make_async_copy(sent, sent, point_send.at[0]).wait()
    for turn in range(3):
        sent = part_in.at[turn, pl.ds(0, devices - 1)]
        pltpu.make_async_copy(sent, sent, part_send.at[turn]).wait()
    def wait_sent(a, b, place):
        for turn, source in enumerate(sources):
            sent = source.at[pl.ds(8, 2)]
            pltpu.make_async_copy(sent, sent, halo_send.at[turn, place]).wait()

    each_beside(wait_sent)


def hand_on(one_ref, two_ref, one_out, two_out, sems):
    copies = [
        pltpu.make_async_copy(one_ref, one_out, sems.at[0]),
        pltpu.make_async_copy(two_ref, two_out, sems.at[1]),
    ]
    for copy in copies:
        copy.start()
    for copy in copies:
        copy.wait()


def shards(wides, narrows, point_owner, point_cell, normals, strip_count, neighbours):
    points = point_cell.shape[0]
    devices = wides * narrows
    slots = 2 * points // wides
    vmem = pl.BlockSpec(memory_space=pltpu.VMEM)
    hbm = pl.BlockSpec(memory_space=pltpu.HBM)
    smem = pl.BlockSpec(memory_space=pltpu.SMEM)
    out = jax.ShapeDtypeStruct((1, 1, 2, 4096), F32)
    results = pl.pallas_call(
        functools.partial(kernel, wides, narrows),
        out_shape=(out, out),
        in_specs=[hbm, hbm, hbm, smem, smem],
        out_specs=(vmem, vmem),
        scratch_shapes=[
            pltpu.VMEM((1, points), jnp.int32),
            pltpu.VMEM((1, points), jnp.int32),
            pltpu.VMEM((3, points), F32),
            pltpu.VMEM((256, 128), BF16),
            pltpu.VMEM((128, 384), BF16),
            pltpu.VMEM((128, 384), BF16),
            pltpu.VMEM((256, 384), BF16),
            pltpu.VMEM((wides, 4, slots), F32),
            pltpu.VMEM((wides, 4, slots), F32),
            pltpu.VMEM((19, 12, 128), F32),
            pltpu.VMEM((19, 12, 128), F32),
            pltpu.VMEM((19, 12, 128), F32),
            pltpu.VMEM((19, 12, 128), F32),
            pltpu.VMEM((3, 2, 128), F32),
            pltpu.VMEM((3, devices, 2, 128), F32),
            pltpu.SemaphoreType.DMA((3,)),
            pltpu.SemaphoreType.DMA((1,)),
            pltpu.SemaphoreType.DMA((1,)),
            pltpu.SemaphoreType.DMA((4, 9)),
            pltpu.SemaphoreType.DMA((4, 9)),
            pltpu.SemaphoreType.DMA((3,)),
            pltpu.SemaphoreType.DMA((3,)),
        ],
        compiler_params=pltpu.CompilerParams(
            collective_id=0, has_side_effects=True, vmem_limit_bytes=56 * 1024 * 1024
        ),
    )(
        point_owner.reshape(1, points), point_cell.reshape(1, points), normals, strip_count, neighbours
    )
    return pl.pallas_call(
        hand_on,
        out_shape=(out, out),
        in_specs=[hbm, hbm],
        out_specs=(hbm, hbm),
        scratch_shapes=[pltpu.SemaphoreType.DMA((2,))],
        compiler_params=pltpu.CompilerParams(vmem_limit_bytes=56 * 1024 * 1024),
    )(*results)


def solution(mesh):
    return jax.shard_map(
        functools.partial(shards, mesh.shape["wide"], mesh.shape["narrow"]),
        mesh=mesh,
        in_specs=(
            P(("wide", "narrow"), None),
            P(("wide", "narrow")),
            P(None, ("wide", "narrow")),
            P(("wide", "narrow")),
            P("wide", "narrow", None, None),
        ),
        out_specs=(P("wide", "narrow", None, None), P("wide", "narrow", None, None)),
        check_vma=False,
    )
```
